256 devices in a mesh: dp: 64 (over z, y, x_hi), mp: 4 (over x_lo, core).
Axes of the slice: x: 4 (x_hi: 2, x_lo: 2; x = x_hi * 2 + x_lo), y: 4, z: 8, core: 2. Of those that a mesh axis runs over, the one named last changes fastest.
Arguments:
- feats: bfloat16 [344064, 512], P('dp', 'mp'), may hold values from -6 to 6
- conv_weight: bfloat16 [1024, 512], P(None, 'mp'), may hold values from -0.1875 to 0.1875
- conv_bias: float32 [512], P('mp'), may hold values from -3 to 3
- norm_gain: float32 [512], P('mp'), may hold values from 0.1 to 1.9
- norm_shift: float32 [512], P('mp'), may hold values from -3 to 3
- lengths: int32 [192], P('dp'), may hold values from 143760 to 287119
- grad_rows: bfloat16 [172032, 512], P('dp', 'mp'), may hold values from -6 to 6
- seg_owner: int32 [1344], P('dp'), may hold values from 0 to 63, as said below
- seg_slot: int32 [1344], P('dp'), may hold values from 0 to 20, as said below
Outputs:
- grad_feats: bfloat16 [344064, 512], P('dp', 'mp')
- grad_weight: float32 [1024, 512], P(None, 'mp')
- grad_bias: float32 [512], P('mp')
- grad_gain: float32 [512], P('mp')
- grad_shift: float32 [512], P('mp')
The draws below stay inside these ranges and needn't reach their ends.
Inputs may be any that keep to these rules, and one draw needn't show every extreme that they name: `seg_owner`: each index of dp sends its frame blocks to distinct owners exactly 2 at a time (one owner fewer at most); every owner receives exactly 21 blocks, one for each of its slots. `seg_slot`: owner and slot together name every block slot of every owner exactly once.
All inputs are finite; a program needn't handle non-finite values.
Results may differ from the reference program's by a relative error of at most 0.0049.
Values may be sent and summed in bfloat16 or wider, within the bound.
No kernel may reach another device: no remote copies, remote signals or barrier semaphores. Data moves between devices by JAX's collectives and lax.ppermute only.
A program may use at most 128 MiB of HBM per device.

```python
import math
import jax
import jax.numpy as jnp
from jax import lax

C = 512
BLOCK = 128
BPU = 7
UTT_DEV = 3
UTTERANCES = 192
N_DP = 64


def route_plan(key):
    total_blocks = UTT_DEV * BPU
    per_peer = max(2, (total_blocks + N_DP - 1) // N_DP)
    groups = (total_blocks + per_peer - 1) // per_peer
    ranking = jax.random.permutation(jax.random.fold_in(key, 11), N_DP).astype(jnp.int32)
    peers = jnp.arange(N_DP, dtype=jnp.int32)
    special = (peers == 1 % N_DP) | (peers == N_DP // 2)
    priority = ranking + jnp.where(special, 0, N_DP).astype(jnp.int32)
    offsets = jnp.argsort(priority)[:groups].astype(jnp.int32)
    rotate = jax.random.randint(jax.random.fold_in(key, 12), (N_DP, 1), 0, total_blocks, dtype=jnp.int32)
    ordering = jax.random.permutation(jax.random.fold_in(key, 13), total_blocks).astype(jnp.int32)
    stride = jax.random.randint(jax.random.fold_in(key, 14), (), 0, total_blocks, dtype=jnp.int32)
    source = jnp.arange(N_DP, dtype=jnp.int32)[:, None]
    position = (jnp.arange(total_blocks, dtype=jnp.int32)[None, :] + rotate) % total_blocks
    owners = (source + offsets[position // per_peer]) % N_DP
    slots = ordering[(position + stride * owners) % total_blocks]
    return (owners.reshape(-1).astype(jnp.int32), slots.reshape(-1).astype(jnp.int32))


def draw_seg_owner(key, part):
    shared = route_plan(key)
    return shared[0]


def draw_seg_slot(key, part):
    shared = route_plan(key)
    return shared[1]


def place_ends(array, own_key, smallest, top_value):
    place = [jax.random.randint(jax.random.fold_in(own_key, axis), (), 0, length) for axis, length in enumerate(array.shape)]
    main_axis = array.shape.index(max(array.shape))
    neighbour = place[:main_axis] + [(place[main_axis] + 1) % array.shape[main_axis]] + place[main_axis + 1:]
    return array.at[tuple(place)].set(smallest).at[tuple(neighbour)].set(top_value)


def shard_levels(key, extent, cuts, low, high):
    level, own = 1.0, jax.random.fold_in(key, 6)
    for dim, shards_of in cuts:
        draws = jnp.exp(jax.random.uniform(jax.random.fold_in(own, dim), (shards_of,), jnp.float32, low / len(cuts), high / len(cuts)))
        level = level * jnp.repeat(draws, extent[dim] // shards_of).reshape([-1 if axis == dim else 1 for axis in range(len(extent))])
    return level


def bell_draw(key, dims, spread, bound, cuts=(), held_as=jnp.bfloat16):
    loudness = shard_levels(key, dims, cuts, -0.22, 0.18) if cuts else 1.0
    values = jax.random.normal(key, dims, jnp.float32) * spread * loudness
    return jnp.minimum(jnp.maximum(values, -bound), bound).astype(held_as)


def setup_inputs(seed: int = 0) -> dict:
    key_of = jax.random.split(jax.random.key(seed), 10)
    feats = bell_draw(key_of[0], (UTTERANCES * 2 * BPU * BLOCK, C), 1.0, 6.0, ((0, 64), (1, 4)))
    conv_weight = bell_draw(key_of[1], (2 * C, C), (2 * C) ** -0.5, 0.1875, ((1, 4),))
    conv_bias = bell_draw(key_of[2], (C,), 0.5, 3.0, ((0, 4),), jnp.float32)
    norm_gain = jnp.clip(1.0 + 0.18 * jax.random.normal(key_of[3], (C,), jnp.float32), 0.1, 1.9)
    norm_shift = bell_draw(key_of[4], (C,), 0.5, 3.0, ((0, 4),), jnp.float32)
    lengths = place_ends(jax.random.randint(key_of[5], (UTTERANCES,), 400 + 320 * (BPU * BLOCK // 2), 400 + 320 * BPU * BLOCK), jax.random.fold_in(key_of[5], 1), 400 + 320 * (BPU * BLOCK // 2), (400 + 320 * BPU * BLOCK) - 1).astype(jnp.int32)
    grad_rows = bell_draw(key_of[6], (N_DP * UTT_DEV * BPU * BLOCK, C), 1.0, 6.0, ((0, 64), (1, 4)))
    seg_owner = draw_seg_owner(jax.random.fold_in(key_of[9], 71), 0)
    seg_slot = draw_seg_slot(jax.random.fold_in(key_of[9], 71), 0)
    return {"feats": feats, "conv_weight": conv_weight, "conv_bias": conv_bias, "norm_gain": norm_gain, "norm_shift": norm_shift, "lengths": lengths, "grad_rows": grad_rows, "seg_owner": seg_owner, "seg_slot": seg_slot}


EPSILON = 1e-05
INV_ROOT_TWO = 0.7071067811865476
INV_ROOT_TAU = 0.3989422804014327

def gelu_slope(value):
    return 0.5 * (1.0 + lax.erf(value * INV_ROOT_TWO)) + value * jnp.exp(-0.5 * value * value) * INV_ROOT_TAU

def owner_pass(carry, inputs):
    conv_weight, conv_bias, norm_gain, norm_shift = carry[2]
    paired, upstream = inputs
    preact = jnp.dot(paired, conv_weight, preferred_element_type=jnp.float32) + conv_bias
    row_mean = lax.optimization_barrier(jnp.mean(preact, axis=1, keepdims=True))
    centred = preact - row_mean
    inv_spread = lax.rsqrt(lax.optimization_barrier(jnp.mean(centred * centred, axis=1, keepdims=True)) + EPSILON)
    normed = centred * inv_spread
    act_in = normed * norm_gain + norm_shift
    grad_act = upstream.astype(jnp.float32) * gelu_slope(act_in)
    grad_normed = grad_act * norm_gain
    grad_pre = inv_spread * (grad_normed - lax.optimization_barrier(jnp.mean(grad_normed, axis=1, keepdims=True)) - normed * lax.optimization_barrier(jnp.mean(grad_normed * normed, axis=1, keepdims=True)))
    grad_low = grad_pre.astype(jnp.bfloat16)
    weight_grad = lax.dot_general(paired, grad_low, (((0,), (0,)), ((), ())), preferred_element_type=jnp.float32)
    vector_grad = jnp.stack([lax.optimization_barrier(jnp.sum(grad_pre, 0)), lax.optimization_barrier(jnp.sum(grad_act * normed, 0)), lax.optimization_barrier(jnp.sum(grad_act, 0))])
    back = lax.dot_general(grad_low, conv_weight, (((1,), (1,)), ((), ())), preferred_element_type=jnp.float32)
    grad_feats = back.reshape(-1, conv_weight.shape[1]).astype(jnp.bfloat16)
    return ((carry[0] + weight_grad, carry[1] + vector_grad, carry[2]), grad_feats)

def reference(feats, conv_weight, conv_bias, norm_gain, norm_shift, lengths, grad_rows, seg_owner, seg_slot):
    channels = conv_weight.shape[1]
    frames = BPU * BLOCK
    destination = (seg_owner * (UTT_DEV * BPU) + seg_slot).astype(jnp.int32)
    blocks = grad_rows.reshape(N_DP * UTT_DEV * BPU, BLOCK * channels)
    placed = jnp.zeros((N_DP * UTT_DEV * BPU, BLOCK * channels), jnp.bfloat16).at[destination].add(blocks)
    valid_frames = (lengths - 400) // 320 + 1
    frame_index = jnp.arange(frames, dtype=jnp.int32)
    keep_mask = (frame_index[None, :] < valid_frames[:, None]).reshape(-1, 1)
    masked = jnp.where(keep_mask, placed.reshape(-1, channels), jnp.zeros((), jnp.bfloat16))
    paired_all = feats.reshape(N_DP, UTT_DEV * frames, 2 * channels)
    masked_all = masked.reshape(N_DP, UTT_DEV * frames, channels)
    start = (jnp.zeros((2 * channels, channels), jnp.float32), jnp.zeros((3, channels), jnp.float32), (conv_weight, conv_bias, norm_gain, norm_shift))
    final, grad_feats = lax.scan(owner_pass, start, (paired_all, masked_all))
    scale = 1.0 / math.sqrt(UTTERANCES * BPU * BLOCK)
    weight_grad = final[0] * scale
    vector_grad = final[1] * scale
    return (grad_feats.reshape(-1, channels), weight_grad, vector_grad[0], vector_grad[1], vector_grad[2])
```

```python
import math

import jax
import jax.numpy as jnp
from jax import lax
from jax.sharding import Mesh, PartitionSpec as P

BLOCK = 128
BPU = 7
SLOTS = 21
PAD = 24
DP = 64
LANES = 128
FRAMES = 32

EPSILON = 1e-05
INV_ROOT_TWO = 0.7071067811865476
INV_ROOT_TAU = 0.3989422804014327


def gelu_slope(value):
    return (
        0.5 * (1.0 + lax.erf(value * INV_ROOT_TWO))
        + value * jnp.exp(-0.5 * value * value) * INV_ROOT_TAU
    )


def swap(value, axis):
    return lax.ppermute(value, axis, [(0, 1), (1, 0)])


def pick(array, index, axis):
    return lax.dynamic_index_in_dim(array, index, axis, keepdims=False)


def ordered(flag, mine, other):
    return jnp.where(flag == 0, mine, other), jnp.where(flag == 0, other, mine)


def route(grad_rows, seg_owner, seg_slot, core):
    pieces = grad_rows.reshape(SLOTS, 2, DP, LANES).transpose(2, 1, 0, 3)
    labels = jnp.pad(
        jnp.stack([seg_owner, seg_slot]).astype(jnp.bfloat16), ((0, 1), (0, LANES - SLOTS))
    )
    outgoing = jnp.concatenate(
        [pieces, jnp.broadcast_to(labels, (DP, 2, PAD - SLOTS, LANES))], axis=2
    )
    spread = lax.all_to_all(outgoing, "dp", split_axis=0, concat_axis=0, tiled=True)
    owner = spread[:, 0, SLOTS, :PAD].astype(jnp.int32)
    slot = spread[:, 0, SLOTS + 1, :PAD].astype(jnp.int32)
    target = jnp.where(jnp.arange(PAD) < SLOTS, owner * PAD + slot, -1).reshape(1, DP * PAD)
    choose = (target == jnp.arange(DP * PAD, dtype=jnp.int32)[:, None]).astype(jnp.bfloat16)
    halves = [
        jnp.dot(
            choose, spread[:, half].reshape(DP * PAD, LANES), preferred_element_type=jnp.float32
        )
        .astype(jnp.bfloat16)
        .reshape(DP, 1, PAD, LANES)
        for half in range(2)
    ]
    sorted_pieces = jnp.concatenate(halves, axis=1).reshape(2 * DP, PAD, LANES)
    arrived = lax.all_to_all(
        sorted_pieces, ("dp", "l"), split_axis=0, concat_axis=0, tiled=True
    ).reshape(2, FRAMES, 2, PAD, LANES)
    mine = pick(arrived, core, 0)
    other = swap(pick(arrived, 1 - core, 0), "c")
    parts = ordered(core, mine, other)
    stacked = jnp.stack(parts, axis=2)[:, :, :, :SLOTS]
    return stacked.transpose(3, 0, 1, 2, 4).reshape(SLOTS * FRAMES, 4 * LANES)


def on_device(
    feats, conv_weight, conv_bias, norm_gain, norm_shift, lengths, grad_rows, seg_owner, seg_slot
):
    link, core = lax.axis_index("l"), lax.axis_index("c")
    group = link * 2 + core
    channels = 4 * LANES

    by_group = feats.reshape(SLOTS, 2, 2, 2 * FRAMES, LANES)
    from_link = swap(pick(by_group, 1 - link, 1), "l")
    both = jnp.stack([pick(by_group, link, 1), from_link])
    kept = pick(both, core, 2)
    from_core = swap(pick(both, 1 - core, 2), "c")
    weight = lax.all_gather(conv_weight, ("l", "c"), axis=1, tiled=True)
    vectors = lax.all_gather(
        jnp.stack([conv_bias, norm_gain, norm_shift]), ("l", "c"), axis=1, tiled=True
    )
    bias, gain, shift = vectors[0], vectors[1], vectors[2]

    upstream = route(grad_rows, seg_owner, seg_slot, core)
    valid_frames = (lengths - 400) // 320 + 1
    frame_index = (
        (jnp.arange(BPU) * BLOCK)[:, None] + (group * FRAMES + jnp.arange(FRAMES))[None, :]
    )
    keep_mask = (frame_index[None] < valid_frames[:, None, None]).reshape(-1, 1)
    upstream = jnp.where(keep_mask, upstream, jnp.zeros((), jnp.bfloat16))

    slices = []
    for part in (0, 1):
        mine = jnp.where(link == part, kept[0], kept[1])
        other = jnp.where(link == part, from_core[0], from_core[1])
        slices.extend(ordered(core, mine, other))
    paired = (
        jnp.stack(slices)
        .reshape(4, SLOTS * FRAMES, 2, LANES)
        .transpose(1, 2, 0, 3)
        .reshape(SLOTS * FRAMES, 2 * channels)
    )

    preact = jnp.dot(paired, weight, preferred_element_type=jnp.float32) + bias
    centred = preact - jnp.mean(preact, axis=1, keepdims=True)
    inv_spread = lax.rsqrt(jnp.mean(centred * centred, axis=1, keepdims=True) + EPSILON)
    normed = centred * inv_spread
    slope = gelu_slope(normed * gain + shift)

    grad_act = upstream.astype(jnp.float32) * slope
    grad_normed = grad_act * gain
    grad_pre = inv_spread * (
        grad_normed
        - jnp.mean(grad_normed, axis=1, keepdims=True)
        - normed * jnp.mean(grad_normed * normed, axis=1, keepdims=True)
    )
    grad_low = grad_pre.astype(jnp.bfloat16)
    weight_grad = lax.dot_general(
        paired, grad_low, (((0,), (0,)), ((), ())), preferred_element_type=jnp.float32
    )
    vector_grad = jnp.stack(
        [jnp.sum(grad_pre, 0), jnp.sum(grad_act * normed, 0), jnp.sum(grad_act, 0)]
    )
    back = lax.dot_general(
        grad_low, weight, (((1,), (1,)), ((), ())), preferred_element_type=jnp.float32
    ).astype(jnp.bfloat16)

    scale = 1.0 / math.sqrt(DP * SLOTS * BLOCK)
    partial = (
        jnp.concatenate([weight_grad, jnp.pad(vector_grad, ((0, 5), (0, 0)))], axis=0)
        .reshape(2 * channels + 8, 2, 2, LANES)
        .transpose(2, 1, 0, 3)
    )
    chip_sum = pick(partial, core, 0) + swap(pick(partial, 1 - core, 0), "c")
    chip_weight = (
        chip_sum[:, : 2 * channels].astype(jnp.bfloat16).reshape(2, DP, 16, LANES)
    ).transpose(1, 0, 2, 3)
    chip_vector = chip_sum[:, 2 * channels :]
    group_vector = pick(chip_vector, link, 0) + swap(pick(chip_vector, 1 - link, 0), "l")
    terms = lax.all_to_all(
        chip_weight.reshape(2 * DP, 16, LANES), ("dp", "l"), split_axis=0, concat_axis=0, tiled=True
    )
    total = (jnp.sum(terms.astype(jnp.float32), axis=0) * scale).astype(jnp.bfloat16)
    high = lax.reduce_precision(group_vector[:3], 8, 7)
    low = group_vector[:3] - high
    pair = jnp.concatenate([high, low]).astype(jnp.bfloat16)
    announce = jnp.concatenate([total, pair, jnp.zeros((2, LANES), jnp.bfloat16)], axis=0)
    heard = lax.all_to_all(
        jnp.broadcast_to(announce, (DP, PAD, LANES)), "dp", split_axis=0, concat_axis=0, tiled=True
    )
    weight_out = heard[:, :16].reshape(2 * channels, LANES).astype(jnp.float32)
    sums = jnp.sum(heard[:, 16:22].astype(jnp.float32), axis=0)
    vector_out = (sums[:3] + sums[3:]) * scale

    by_slice = back.reshape(SLOTS * FRAMES, 2, 2, 2, LANES).transpose(3, 2, 0, 1, 4)
    own_rows = pick(by_slice, core, 0)
    core_rows = swap(pick(by_slice, 1 - core, 0), "c")
    chip_rows = jnp.stack([own_rows, core_rows])
    here = pick(chip_rows, link, 1)
    there = swap(pick(chip_rows, 1 - link, 1), "l")
    groups = []
    for part in (0, 1):
        rows = jnp.where(link == part, here, there)
        groups.extend(ordered(core, rows[0], rows[1]))
    grad_feats = (
        jnp.stack(groups)
        .reshape(4, SLOTS, 2 * FRAMES, LANES)
        .transpose(1, 0, 2, 3)
        .reshape(feats.shape)
    )
    return (grad_feats, weight_out, vector_out[0], vector_out[1], vector_out[2])


def solution(mesh):
    grid = Mesh(mesh.devices.reshape(DP, 2, 2), ("dp", "l", "c"))
    mp = ("l", "c")
    placed = (
        P("dp", mp),
        P(None, mp),
        P(mp),
        P(mp),
        P(mp),
        P("dp"),
        P("dp", mp),
        P("dp"),
        P("dp"),
    )
    return jax.shard_map(
        on_device,
        mesh=grid,
        in_specs=placed,
        out_specs=(P("dp", mp), P(None, mp), P(mp), P(mp), P(mp)),
        check_vma=False,
    )
```

```python
import math

import jax
import jax.numpy as jnp
import numpy as np
from jax import lax
from jax.experimental import pallas as pl
from jax.experimental.pallas import tpu as pltpu
from jax.sharding import Mesh, PartitionSpec as P

BLOCK = 128
BPU = 7
SLOTS = 21
PAD = 24
DP = 64
LANES = 128
FRAMES = 32

VMEM = 48 * 1024 * 1024

EPSILON = 1e-05
INV_ROOT_TWO = 0.7071067811865476
INV_ROOT_TAU = 0.3989422804014327


def gelu_slope(value):
    return (
        0.5 * (1.0 + lax.erf(value * INV_ROOT_TWO))
        + value * jnp.exp(-0.5 * value * value) * INV_ROOT_TAU
    )


def swap(value, axis):
    return lax.ppermute(value, axis, [(0, 1), (1, 0)])


def pick(array, index, axis):
    return lax.dynamic_index_in_dim(array, index, axis, keepdims=False)


def ordered(flag, mine, other):
    return jnp.where(flag == 0, mine, other), jnp.where(flag == 0, other, mine)


def lay_out_kernel(rows_ref, owner_ref, slot_ref, out_ref, wide_ref):
    wide_ref[: SLOTS * BLOCK] = rows_ref[...].astype(jnp.float32)
    lane = lax.broadcasted_iota(jnp.int32, (1, LANES), 1)
    for place, label_ref in enumerate((owner_ref, slot_ref)):
        label = jnp.zeros((1, LANES), jnp.int32)
        for block in range(SLOTS):
            label = jnp.where(lane == block, label_ref[block], label)
        start = (SLOTS + place) * BLOCK
        wide_ref[start : start + BLOCK] = jnp.broadcast_to(label.astype(jnp.float32), (BLOCK, LANES))
    wide_ref[(SLOTS + 2) * BLOCK :] = jnp.zeros((BLOCK, LANES), jnp.float32)
    for half in range(2):
        for frame in range(DP):
            column = wide_ref[pl.ds(half * DP + frame, PAD, stride=BLOCK), :]
            out_ref[frame, half] = column.astype(jnp.bfloat16)


def lay_out(grad_rows, seg_owner, seg_slot):
    return pl.pallas_call(
        lay_out_kernel,
        out_shape=jax.ShapeDtypeStruct((DP, 2, PAD, LANES), jnp.bfloat16),
        in_specs=[
            pl.BlockSpec(memory_space=pltpu.VMEM),
            pl.BlockSpec(memory_space=pltpu.SMEM),
            pl.BlockSpec(memory_space=pltpu.SMEM),
        ],
        scratch_shapes=[pltpu.VMEM((PAD * BLOCK, LANES), jnp.float32)],
        compiler_params=pltpu.CompilerParams(vmem_limit_bytes=VMEM),
        cost_estimate=pl.CostEstimate(flops=0, bytes_accessed=1500000, transcendentals=0),
    )(grad_rows, seg_owner, seg_slot)


def permute_kernel(lane_ref, spread_ref, out_ref, rows_ref, labels_ref, target_ref):
    step = pl.program_id(0)
    owners = out_ref.shape[0]
    tile = owners * PAD
    width = DP * PAD

    @pl.when(step == 0)
    def _():
        for half in range(2):
            values = spread_ref[:, half].astype(jnp.float32).reshape(width, LANES)
            rows_ref[:, half * LANES : (half + 1) * LANES] = values.astype(jnp.bfloat16)
        labels_ref[...] = spread_ref[:, 0, PAD - 8 :].astype(jnp.float32).reshape(DP * 8, LANES)
        block = lane_ref[0:1, :]
        source = lane_ref[1:2, :]
        repeat = jnp.where(
            lax.broadcasted_iota(jnp.int32, (LANES, width), 0) == block, 1.0, 0.0
        ).astype(jnp.bfloat16)
        own_row = lax.broadcasted_iota(jnp.int32, (DP, width), 0) == source
        found = []
        for row in (SLOTS, SLOTS + 1):
            label = labels_ref[pl.ds(row - (PAD - 8), DP, stride=8), :].astype(jnp.bfloat16)
            spun = jnp.dot(label, repeat, preferred_element_type=jnp.float32)
            found.append(jnp.sum(jnp.where(own_row, spun, 0.0), axis=0, keepdims=True))
        target = (found[0] * PAD + found[1]).astype(jnp.int32)
        target_ref[...] = jnp.where(block < SLOTS, target, -1)

    wanted = step * tile + lax.broadcasted_iota(jnp.int32, (tile, DP * PAD), 0)
    choose = jnp.where(target_ref[...] == wanted, 1.0, 0.0).astype(jnp.bfloat16)
    moved = jnp.dot(choose, rows_ref[...], preferred_element_type=jnp.float32)
    for half in range(2):
        values = moved[:, half * LANES : (half + 1) * LANES].reshape(owners, PAD, LANES)
        out_ref[:, half] = values.astype(jnp.bfloat16)


def permute_pieces(spread):
    steps = 4
    width = DP * PAD
    lanes = np.arange(width, dtype=np.int32)
    places = np.concatenate([np.stack([lanes % PAD, lanes // PAD]), np.zeros((6, width), np.int32)])
    return pl.pallas_call(
        permute_kernel,
        grid=(steps,),
        out_shape=jax.ShapeDtypeStruct(spread.shape, jnp.bfloat16),
        in_specs=[
            pl.BlockSpec((8, width), lambda i: (0, 0)),
            pl.BlockSpec(spread.shape, lambda i: (0, 0, 0, 0)),
        ],
        out_specs=pl.BlockSpec((DP // steps, 2, PAD, LANES), lambda i: (i, 0, 0, 0)),
        scratch_shapes=[
            pltpu.VMEM((width, 2 * LANES), jnp.bfloat16),
            pltpu.VMEM((DP * 8, LANES), jnp.float32),
            pltpu.VMEM((1, width), jnp.int32),
        ],
        compiler_params=pltpu.CompilerParams(vmem_limit_bytes=VMEM),
        cost_estimate=pl.CostEstimate(
            flops=4 * 2 * width * width * 2 * LANES, bytes_accessed=1600000, transcendentals=0
        ),
    )(places, spread)


def parameter(terms, which):
    terms = terms.astype(jnp.float32)
    return sum(terms[3 * part + which : 3 * part + which + 1] for part in range(3))


def forward_kernel(
    place_ref, lengths_ref, feats_ref, link_ref, beside_ref, weight_ref,
    paired_ref, slope_ref, normed_ref, inv_ref, rows_ref, wide_ref,
):
    step = pl.program_id(0)
    link, core = place_ref[0], place_ref[1]
    blocks = SLOTS * 2 * FRAMES
    rows, channels = slope_ref.shape
    frames = rows // PAD

    @pl.when(step == 0)
    def _():
        sources = (
            (link * 2 + core, feats_ref[:, 0]),
            ((1 - link) * 2 + core, link_ref[:, 0]),
            (link * 2 + 1 - core, beside_ref[0]),
            ((1 - link) * 2 + 1 - core, beside_ref[1]),
        )
        for place, value in sources:
            rows_ref[place, :blocks] = value.astype(jnp.float32).reshape(blocks, LANES)
        rows_ref[:, blocks:] = jnp.zeros((4, (PAD - SLOTS) * 2 * FRAMES, LANES), jnp.float32)

    for frame in range(frames):
        for tap in range(2):
            for piece in range(4):
                start = 2 * (step * frames + frame) + tap
                column = tap * channels + piece * LANES
                wide_ref[frame * PAD : (frame + 1) * PAD, column : column + LANES] = rows_ref[
                    piece, pl.ds(start, PAD, stride=2 * FRAMES), :
                ]
    paired = wide_ref[...].astype(jnp.bfloat16)
    paired_ref[...] = paired
    terms = weight_ref[2 * channels :]
    preact = jnp.dot(paired, weight_ref[: 2 * channels], preferred_element_type=jnp.float32)
    preact = preact + parameter(terms, 0)
    centred = preact - jnp.sum(preact, axis=1, keepdims=True) * (1.0 / channels)
    spread = jnp.sum(centred * centred, axis=1, keepdims=True) * (1.0 / channels)
    inv_spread = lax.rsqrt(spread + EPSILON)
    normed = centred * inv_spread
    slope = gelu_slope(normed * parameter(terms, 1) + parameter(terms, 2))
    slot = lax.broadcasted_iota(jnp.int32, (PAD, 1), 0)
    limit = jnp.zeros((PAD, 1), jnp.int32)
    for index in range(SLOTS):
        valid = lax.div(lengths_ref[index // BPU] - 400, 320) + 1
        here = valid - (index % BPU) * BLOCK - (link * 2 + core) * FRAMES
        limit = jnp.where(slot == index, here, limit)
    limits = jnp.concatenate([limit - frame for frame in range(frames)], axis=0)
    slope_ref[...] = jnp.where(limits > step * frames, slope, 0.0)
    normed_ref[...] = normed
    inv_ref[...] = jnp.broadcast_to(inv_spread, inv_ref.shape)


def forward(link, core, lengths, by_group, from_link, from_core, weight):
    steps = 4
    rows = FRAMES * PAD
    channels = weight.shape[1]
    tile = rows // steps
    group_block = (SLOTS, 1, 2 * FRAMES, LANES)
    wide = jax.ShapeDtypeStruct((rows, channels), jnp.float32)
    return pl.pallas_call(
        forward_kernel,
        grid_spec=pltpu.PrefetchScalarGridSpec(
            num_scalar_prefetch=2,
            grid=(steps,),
            in_specs=[
                pl.BlockSpec(group_block, lambda i, place, _: (0, 2 * place[0] + place[1], 0, 0)),
                pl.BlockSpec(group_block, lambda i, place, _: (0, place[1], 0, 0)),
                pl.BlockSpec(from_core.shape, lambda i, place, _: (0, 0, 0, 0)),
                pl.BlockSpec(weight.shape, lambda i, place, _: (0, 0)),
            ],
            out_specs=(
                pl.BlockSpec((tile, 2 * channels), lambda i, place, _: (i, 0)),
                pl.BlockSpec((tile, channels), lambda i, place, _: (i, 0)),
                pl.BlockSpec((tile, channels), lambda i, place, _: (i, 0)),
                pl.BlockSpec((tile, LANES), lambda i, place, _: (i, 0)),
            ),
            scratch_shapes=[
                pltpu.VMEM((4, PAD * 2 * FRAMES, LANES), jnp.float32),
                pltpu.VMEM((tile, 2 * channels), jnp.float32),
            ],
        ),
        out_shape=(
            jax.ShapeDtypeStruct((rows, 2 * channels), jnp.bfloat16),
            wide,
            wide,
            jax.ShapeDtypeStruct((rows, LANES), jnp.float32),
        ),
        compiler_params=pltpu.CompilerParams(vmem_limit_bytes=VMEM),
        cost_estimate=pl.CostEstimate(
            flops=3 * 4 * rows * channels * channels,
            bytes_accessed=8000000,
            transcendentals=2 * rows * channels,
        ),
    )(jnp.stack([link, core]), lengths, by_group, from_link, from_core, weight)


def backward_kernel(
    core_ref, own_ref, other_ref, slope_ref, normed_ref, inv_ref, gain_ref, paired_ref,
    low_ref, keep_ref, send_ref, sums_ref,
):
    step = pl.program_id(0)
    rows = slope_ref.shape[0]
    first = core_ref[0] == 0
    columns = []
    for link in range(2):
        own = own_ref[0, :, link].astype(jnp.float32).reshape(rows, LANES)
        other = other_ref[:, link].astype(jnp.float32).reshape(rows, LANES)
        columns.append(jnp.where(first, own, other))
        columns.append(jnp.where(first, other, own))
    upstream = jnp.concatenate(columns, axis=1)
    normed = normed_ref[...]
    grad_act = upstream * slope_ref[...]
    weighted = grad_act * normed
    gain = parameter(gain_ref[...], 1)
    grad_normed = grad_act * gain
    channels = normed.shape[1]
    grad_mean = jnp.sum(grad_normed, axis=1, keepdims=True) * (1.0 / channels)
    cross_mean = jnp.sum(weighted * gain, axis=1, keepdims=True) * (1.0 / channels)
    grad_pre = inv_ref[:, :1] * (grad_normed - grad_mean - normed * cross_mean)
    low_ref[pl.ds(pl.multiple_of(step * rows, 16), rows), :] = grad_pre.astype(jnp.bfloat16)
    sums = jnp.concatenate(
        [
            jnp.sum(grad_pre, axis=0, keepdims=True),
            jnp.sum(weighted, axis=0, keepdims=True),
            jnp.sum(grad_act, axis=0, keepdims=True),
            jnp.zeros((5, channels), jnp.float32),
        ],
        axis=0,
    )

    @pl.when(step == 0)
    def _():
        sums_ref[...] = sums

    @pl.when(step > 0)
    def _():
        sums_ref[...] += sums

    @pl.when(step == pl.num_programs(0) - 1)
    def _():
        depth = paired_ref.shape[1]
        for target_ref, which in ((send_ref, 1 - core_ref[0]), (keep_ref, core_ref[0])):
            places = [pl.ds(pl.multiple_of((2 * link + which) * LANES, LANES), LANES) for link in range(2)]
            columns = jnp.concatenate([low_ref[:, place] for place in places], axis=1)
            product = lax.dot_general(
                paired_ref[...], columns, (((0,), (0,)), ((), ())),
                preferred_element_type=jnp.float32,
            )
            for link in range(2):
                target_ref[link, :depth] = product[:, link * LANES : (link + 1) * LANES]
                target_ref[link, depth:] = sums_ref[:, places[link]]


def backward(core, own, other, slope, normed, inv_spread, gain, paired):
    steps = 4
    rows, channels = normed.shape
    depth = paired.shape[1]
    tile = rows // steps
    frames = FRAMES // steps
    half = jax.ShapeDtypeStruct((2, depth + 8, LANES), jnp.float32)
    return pl.pallas_call(
        backward_kernel,
        grid_spec=pltpu.PrefetchScalarGridSpec(
            num_scalar_prefetch=1,
            grid=(steps,),
            in_specs=[
                pl.BlockSpec((1, frames, 2, PAD, LANES), lambda i, core: (core[0], i, 0, 0, 0)),
                pl.BlockSpec((frames, 2, PAD, LANES), lambda i, core: (i, 0, 0, 0)),
                pl.BlockSpec((tile, channels), lambda i, core: (i, 0)),
                pl.BlockSpec((tile, channels), lambda i, core: (i, 0)),
                pl.BlockSpec((tile, LANES), lambda i, core: (i, 0)),
                pl.BlockSpec((16, channels), lambda i, core: (depth // 16, 0)),
                pl.BlockSpec((rows, depth), lambda i, core: (0, 0)),
            ],
            out_specs=(
                pl.BlockSpec((rows, channels), lambda i, core: (0, 0)),
                pl.BlockSpec(half.shape, lambda i, core: (0, 0, 0)),
                pl.BlockSpec(half.shape, lambda i, core: (0, 0, 0)),
            ),
            scratch_shapes=[pltpu.VMEM((8, channels), jnp.float32)],
        ),
        out_shape=(jax.ShapeDtypeStruct((rows, channels), jnp.bfloat16), half, half),
        compiler_params=pltpu.CompilerParams(vmem_limit_bytes=VMEM),
        cost_estimate=pl.CostEstimate(
            flops=2 * rows * depth * channels, bytes_accessed=9000000, transcendentals=0
        ),
    )(core.reshape(1), own, other, slope, normed, inv_spread, gain, paired)


def input_kernel(core_ref, low_ref, weight_ref, keep_ref, send_ref):
    low = low_ref[...]
    for target_ref, which in ((send_ref, 1 - core_ref[0]), (keep_ref, core_ref[0])):
        for tap in range(2):
            rows = [
                weight_ref[pl.ds(pl.multiple_of((4 * tap + 2 * link + which) * LANES, LANES), LANES), :]
                for link in range(2)
            ]
            product = lax.dot_general(
                low, jnp.concatenate(rows, axis=0), (((1,), (1,)), ((), ())),
                preferred_element_type=jnp.float32,
            ).astype(jnp.bfloat16)
            for link in range(2):
                target_ref[link, tap] = product[:, link * LANES : (link + 1) * LANES]


def input_gradient(core, low, weight):
    rows = low.shape[0]
    half = jax.ShapeDtypeStruct((2, 2, rows, LANES), jnp.bfloat16)
    return pl.pallas_call(
        input_kernel,
        out_shape=(half, half),
        in_specs=[
            pl.BlockSpec(memory_space=pltpu.SMEM),
            pl.BlockSpec(memory_space=pltpu.VMEM),
            pl.BlockSpec(memory_space=pltpu.VMEM),
        ],
        out_specs=(pl.BlockSpec(memory_space=pltpu.VMEM),) * 2,
        compiler_params=pltpu.CompilerParams(vmem_limit_bytes=VMEM),
        cost_estimate=pl.CostEstimate(
            flops=4 * rows * weight.shape[1] * weight.shape[1],
            bytes_accessed=3500000,
            transcendentals=0,
        ),
    )(core.reshape(1), low, weight)


def chip_kernel(keep_ref, other_ref, weight_ref, vector_ref):
    total = keep_ref[0] + other_ref[0]
    depth = total.shape[0] - 8
    weight_ref[:, 0] = total[:depth].reshape(DP, depth // DP, LANES).astype(jnp.bfloat16)
    vector_ref[0] = total[depth:]


def chip_total(keep, other):
    depth = keep.shape[1] - 8
    return pl.pallas_call(
        chip_kernel,
        grid=(2,),
        out_shape=(
            jax.ShapeDtypeStruct((DP, 2, depth // DP, LANES), jnp.bfloat16),
            jax.ShapeDtypeStruct((2, 8, LANES), jnp.float32),
        ),
        in_specs=[pl.BlockSpec((1, depth + 8, LANES), lambda i: (i, 0, 0))] * 2,
        out_specs=(
            pl.BlockSpec((DP, 1, depth // DP, LANES), lambda i: (0, i, 0, 0)),
            pl.BlockSpec((1, 8, LANES), lambda i: (i, 0, 0)),
        ),
        compiler_params=pltpu.CompilerParams(vmem_limit_bytes=VMEM),
        cost_estimate=pl.CostEstimate(
            flops=2 * depth * LANES, bytes_accessed=2700000, transcendentals=0
        ),
    )(keep, other)


def route(grad_rows, seg_owner, seg_slot):
    outgoing = lay_out(grad_rows, seg_owner, seg_slot)
    spread = lax.all_to_all(outgoing, "dp", split_axis=0, concat_axis=0, tiled=True)
    sorted_pieces = permute_pieces(spread).reshape(2 * DP, PAD, LANES)
    arrived = lax.all_to_all(
        sorted_pieces, ("dp", "l"), split_axis=0, concat_axis=0, tiled=True
    ).reshape(2, FRAMES, 2, PAD, LANES)
    return arrived, sorted_pieces


def gather_parameters(conv_weight, vectors):
    high = lax.reduce_precision(vectors, 8, 7)
    middle = lax.reduce_precision(vectors - high, 8, 7)
    terms = jnp.concatenate([high, middle, vectors - high - middle]).astype(jnp.bfloat16)
    packed = jnp.concatenate([conv_weight, jnp.pad(terms, ((0, 7), (0, 0)))], axis=0)
    return lax.all_gather(packed, ("l", "c"), axis=1, tiled=True)


def on_device(
    feats, conv_weight, conv_bias, norm_gain, norm_shift, lengths, grad_rows, seg_owner, seg_slot
):
    link, core = lax.axis_index("l"), lax.axis_index("c")
    channels = 4 * LANES

    own, sorted_pieces = route(grad_rows, seg_owner, seg_slot)

    by_group = feats.reshape(SLOTS, 2, 2, 2 * FRAMES, LANES)
    from_link = swap(pick(by_group, 1 - link, 1), "l")
    from_link, _ = lax.optimization_barrier((from_link, sorted_pieces))
    both = jnp.stack([pick(by_group, link, 1), from_link])
    from_core = swap(pick(both, 1 - core, 2), "c")
    weight = gather_parameters(conv_weight, jnp.stack([conv_bias, norm_gain, norm_shift]))
    paired, slope, normed, inv_spread = forward(
        link, core, lengths, by_group.reshape(SLOTS, 4, 2 * FRAMES, LANES), from_link, from_core,
        weight,
    )

    leaving, _ = lax.optimization_barrier((pick(own, 1 - core, 0), paired))
    other = swap(leaving, "c")

    low, keep, send = backward(
        core, own, other, slope, normed, inv_spread, weight, paired
    )
    chip_weight, chip_vector = chip_total(keep, swap(send, "c"))

    scale = 1.0 / math.sqrt(DP * SLOTS * BLOCK)
    group_vector = pick(chip_vector, link, 0) + swap(pick(chip_vector, 1 - link, 0), "l")
    terms = lax.all_to_all(
        chip_weight.reshape(2 * DP, 16, LANES), ("dp", "l"), split_axis=0, concat_axis=0, tiled=True
    )
    total = (jnp.sum(terms.astype(jnp.float32), axis=0) * scale).astype(jnp.bfloat16)
    high = lax.reduce_precision(group_vector[:3], 8, 7)
    rest = group_vector[:3] - high
    pair = jnp.concatenate([high, rest]).astype(jnp.bfloat16)
    announce = jnp.concatenate([total, pair, jnp.zeros((2, LANES), jnp.bfloat16)], axis=0)
    heard = lax.all_to_all(
        jnp.broadcast_to(announce, (DP, PAD, LANES)), "dp", split_axis=0, concat_axis=0, tiled=True
    )
    weight_out = heard[:, :16].reshape(2 * channels, LANES).astype(jnp.float32)
    sums = jnp.sum(heard[:, 16:22].astype(jnp.float32), axis=0)
    vector_out = (sums[:3] + sums[3:]) * scale

    own_rows, leaving_rows = input_gradient(core, low, weight)
    chip_rows = jnp.stack([own_rows, swap(leaving_rows, "c")])
    here = pick(chip_rows, link, 1)
    there = swap(pick(chip_rows, 1 - link, 1), "l")
    groups = []
    for part in (0, 1):
        rows = jnp.where(link == part, here, there)
        groups.extend(ordered(core, rows[0], rows[1]))
    grad_feats = (
        jnp.stack(groups)
        .reshape(4, 2, FRAMES, PAD, LANES)[:, :, :, :SLOTS]
        .transpose(3, 0, 2, 1, 4)
        .reshape(feats.shape)
    )
    return (grad_feats, weight_out, vector_out[0], vector_out[1], vector_out[2])


def solution(mesh):
    grid = Mesh(mesh.devices.reshape(DP, 2, 2), ("dp", "l", "c"))
    mp = ("l", "c")
    placed = (
        P("dp", mp),
        P(None, mp),
        P(mp),
        P(mp),
        P(mp),
        P("dp"),
        P("dp", mp),
        P("dp"),
        P("dp"),
    )
    return jax.shard_map(
        on_device,
        mesh=grid,
        in_specs=placed,
        out_specs=(P("dp", mp), P(None, mp), P(mp), P(mp), P(mp)),
        check_vma=False,
    )
```

```python
import math

import jax
import jax.numpy as jnp
import numpy as np
from jax import lax
from jax.experimental import pallas as pl
from jax.experimental.pallas import tpu as pltpu
from jax.sharding import Mesh, PartitionSpec as P

BLOCK = 128
BPU = 7
SLOTS = 21
PAD = 24
DP = 64
LANES = 128
FRAMES = 32

MIB = 1024 * 1024
VMEM = 28 * MIB
ALL_VMEM = 60 * MIB

EPSILON = 1e-05
INV_ROOT_TWO = 0.7071067811865476
INV_ROOT_TAU = 0.3989422804014327


def gelu_slope(value):
    return (
        0.5 * (1.0 + lax.erf(value * INV_ROOT_TWO))
        + value * jnp.exp(-0.5 * value * value) * INV_ROOT_TAU
    )


def swap(value, axis):
    return lax.ppermute(value, axis, [(0, 1), (1, 0)])


def pick(array, index, axis):
    return lax.dynamic_index_in_dim(array, index, axis, keepdims=False)


def ordered(flag, mine, other):
    return jnp.where(flag == 0, mine, other), jnp.where(flag == 0, other, mine)


def lay_out_kernel(
    rows_ref, owner_ref, slot_ref, out_ref, held_ref, owners_ref, slots_ref, wide_ref, sems
):
    copies = [
        pltpu.make_async_copy(rows_ref, held_ref, sems.at[0]),
        pltpu.make_async_copy(owner_ref, owners_ref, sems.at[1]),
        pltpu.make_async_copy(slot_ref, slots_ref, sems.at[2]),
    ]
    for copy in copies:
        copy.start()
    wide_ref[(SLOTS + 2) * BLOCK :] = jnp.zeros((BLOCK, LANES), jnp.float32)
    lane = lax.broadcasted_iota(jnp.int32, (1, LANES), 1)
    for place, label_ref in enumerate((owners_ref, slots_ref)):
        copies[1 + place].wait()
        label = jnp.zeros((1, LANES), jnp.int32)
        for block in range(SLOTS):
            label = jnp.where(lane == block, label_ref[block], label)
        start = (SLOTS + place) * BLOCK
        wide_ref[start : start + BLOCK] = jnp.broadcast_to(
            label.astype(jnp.float32), (BLOCK, LANES)
        )
    copies[0].wait()
    wide_ref[: SLOTS * BLOCK] = held_ref[...].astype(jnp.float32)
    for half in range(2):
        for frame in range(DP):
            column = wide_ref[pl.ds(half * DP + frame, PAD, stride=BLOCK), :]
            out_ref[frame, half] = column.astype(jnp.bfloat16)


def lay_out(grad_rows, seg_owner, seg_slot):
    return pl.pallas_call(
        lay_out_kernel,
        out_shape=jax.ShapeDtypeStruct((DP, 2, PAD, LANES), jnp.bfloat16),
        in_specs=[pl.BlockSpec(memory_space=pl.ANY)] * 3,
        scratch_shapes=[
            pltpu.VMEM((SLOTS * BLOCK, LANES), jnp.bfloat16),
            pltpu.SMEM((SLOTS,), jnp.int32),
            pltpu.SMEM((SLOTS,), jnp.int32),
            pltpu.VMEM((PAD * BLOCK, LANES), jnp.float32),
            pltpu.SemaphoreType.DMA((3,)),
        ],
        compiler_params=pltpu.CompilerParams(vmem_limit_bytes=ALL_VMEM),
        cost_estimate=pl.CostEstimate(flops=0, bytes_accessed=1500000, transcendentals=0),
    )(grad_rows, seg_owner, seg_slot)


def permute_kernel(lane_ref, spread_ref, out_ref, rows_ref, labels_ref, target_ref):
    step = pl.program_id(0)
    owners = out_ref.shape[0]
    tile = owners * PAD
    width = DP * PAD

    @pl.when(step == 0)
    def _():
        for half in range(2):
            values = spread_ref[:, half].astype(jnp.float32).reshape(width, LANES)
            rows_ref[:, half * LANES : (half + 1) * LANES] = values.astype(jnp.bfloat16)
        labels_ref[...] = spread_ref[:, 0, PAD - 8 :].astype(jnp.float32).reshape(DP * 8, LANES)
        block = lane_ref[0:1, :]
        source = lane_ref[1:2, :]
        repeat = jnp.where(
            lax.broadcasted_iota(jnp.int32, (LANES, width), 0) == block, 1.0, 0.0
        ).astype(jnp.bfloat16)
        own_row = lax.broadcasted_iota(jnp.int32, (DP, width), 0) == source
        found = []
        for row in (SLOTS, SLOTS + 1):
            label = labels_ref[pl.ds(row - (PAD - 8), DP, stride=8), :].astype(jnp.bfloat16)
            spun = jnp.dot(label, repeat, preferred_element_type=jnp.float32)
            found.append(jnp.sum(jnp.where(own_row, spun, 0.0), axis=0, keepdims=True))
        target = (found[0] * PAD + found[1]).astype(jnp.int32)
        target_ref[...] = jnp.where(block < SLOTS, target, -1)

    wanted = step * tile + lax.broadcasted_iota(jnp.int32, (tile, DP * PAD), 0)
    choose = jnp.where(target_ref[...] == wanted, 1.0, 0.0).astype(jnp.bfloat16)
    moved = jnp.dot(choose, rows_ref[...], preferred_element_type=jnp.float32)
    for half in range(2):
        values = moved[:, half * LANES : (half + 1) * LANES].reshape(owners, PAD, LANES)
        out_ref[:, half] = values.astype(jnp.bfloat16)


def permute_pieces(spread):
    steps = 4
    width = DP * PAD
    lanes = np.arange(width, dtype=np.int32)
    places = np.concatenate([np.stack([lanes % PAD, lanes // PAD]), np.zeros((6, width), np.int32)])
    return pl.pallas_call(
        permute_kernel,
        grid=(steps,),
        out_shape=jax.ShapeDtypeStruct(spread.shape, jnp.bfloat16),
        in_specs=[
            pl.BlockSpec((8, width), lambda i: (0, 0)),
            pl.BlockSpec(spread.shape, lambda i: (0, 0, 0, 0)),
        ],
        out_specs=pl.BlockSpec((DP // steps, 2, PAD, LANES), lambda i: (i, 0, 0, 0)),
        scratch_shapes=[
            pltpu.VMEM((width, 2 * LANES), jnp.bfloat16),
            pltpu.VMEM((DP * 8, LANES), jnp.float32),
            pltpu.VMEM((1, width), jnp.int32),
        ],
        compiler_params=pltpu.CompilerParams(vmem_limit_bytes=VMEM),
        cost_estimate=pl.CostEstimate(
            flops=4 * 2 * width * width * 2 * LANES, bytes_accessed=1600000, transcendentals=0
        ),
    )(places, spread)


def parameter(terms, which):
    terms = terms.astype(jnp.float32)
    return sum(terms[3 * part + which : 3 * part + which + 1] for part in range(3))


def forward_kernel(
    place_ref, lengths_ref, feats_ref, packed_ref, link_ref, beside_ref,
    transposed_ref, slope_ref, normed_ref, weight_ref, rows_ref, wide_ref,
):
    step = pl.program_id(0)
    link, core = place_ref[0], place_ref[1]
    blocks = SLOTS * 2 * FRAMES
    rows, channels = normed_ref.shape
    frames = rows // PAD

    @pl.when(step == 0)
    def _():
        sources = (
            (link * 2 + core, feats_ref[:, 0].astype(jnp.float32).reshape(blocks, LANES), packed_ref[...]),
            (
                (1 - link) * 2 + core,
                link_ref[pl.ds(pl.multiple_of(core * blocks, 16), blocks), :].astype(jnp.float32),
                link_ref[2 * blocks :],
            ),
            (link * 2 + 1 - core, beside_ref[0, :blocks].astype(jnp.float32), beside_ref[0, blocks:]),
            (
                (1 - link) * 2 + 1 - core,
                beside_ref[1, :blocks].astype(jnp.float32),
                beside_ref[1, blocks:],
            ),
        )
        for place, value, weight in sources:
            rows_ref[place, :blocks] = value
            weight_ref[:, pl.ds(pl.multiple_of(place * LANES, LANES), LANES)] = weight
        rows_ref[:, blocks:] = jnp.zeros((4, (PAD - SLOTS) * 2 * FRAMES, LANES), jnp.float32)

    for frame in range(frames):
        for tap in range(2):
            for piece in range(4):
                start = 2 * (step * frames + frame) + tap
                column = tap * channels + piece * LANES
                wide_ref[frame * PAD : (frame + 1) * PAD, column : column + LANES] = rows_ref[
                    piece, pl.ds(start, PAD, stride=2 * FRAMES), :
                ]
    paired = wide_ref[...].astype(jnp.bfloat16)
    transposed_ref[...] = paired.T
    terms = weight_ref[2 * channels :]
    preact = jnp.dot(paired, weight_ref[: 2 * channels], preferred_element_type=jnp.float32)
    preact = preact + parameter(terms, 0)
    centred = preact - jnp.sum(preact, axis=1, keepdims=True) * (1.0 / channels)
    spread = jnp.sum(centred * centred, axis=1, keepdims=True) * (1.0 / channels)
    inv_spread = lax.rsqrt(spread + EPSILON)
    normed = centred * inv_spread
    slope = gelu_slope(normed * parameter(terms, 1) + parameter(terms, 2))
    slot = lax.broadcasted_iota(jnp.int32, (PAD, 1), 0)
    limit = jnp.zeros((PAD, 1), jnp.int32)
    for index in range(SLOTS):
        valid = lax.div(lengths_ref[index // BPU] - 400, 320) + 1
        here = valid - (index % BPU) * BLOCK - (link * 2 + core) * FRAMES
        limit = jnp.where(slot == index, here, limit)
    limits = jnp.concatenate([limit - frame for frame in range(frames)], axis=0)
    slope_ref[:, :channels] = jnp.where(limits > step * frames, slope, 0.0)
    slope_ref[:, channels:] = jnp.broadcast_to(inv_spread, (rows, LANES))
    normed_ref[...] = normed


def forward(link, core, lengths, feats, packed, from_link, from_core):
    steps = 2
    rows = FRAMES * PAD
    channels = 4 * LANES
    tile = rows // steps
    return pl.pallas_call(
        forward_kernel,
        grid_spec=pltpu.PrefetchScalarGridSpec(
            num_scalar_prefetch=2,
            grid=(steps,),
            in_specs=[
                pl.BlockSpec(
                    (SLOTS, 1, 2 * FRAMES, LANES),
                    lambda i, place, _: (0, 2 * place[0] + place[1], 0, 0),
                ),
                pl.BlockSpec(packed.shape, lambda i, place, _: (0, 0)),
                pl.BlockSpec(from_link.shape, lambda i, place, _: (0, 0)),
                pl.BlockSpec(from_core.shape, lambda i, place, _: (0, 0, 0)),
            ],
            out_specs=(
                pl.BlockSpec((2 * channels, tile), lambda i, place, _: (0, i)),
                pl.BlockSpec((tile, channels + LANES), lambda i, place, _: (i, 0)),
                pl.BlockSpec((tile, channels), lambda i, place, _: (i, 0)),
                pl.BlockSpec((packed.shape[0], channels), lambda i, place, _: (0, 0)),
            ),
            scratch_shapes=[
                pltpu.VMEM((4, PAD * 2 * FRAMES, LANES), jnp.float32),
                pltpu.VMEM((tile, 2 * channels), jnp.float32),
            ],
        ),
        out_shape=(
            pltpu.HBM((2 * channels, rows), jnp.bfloat16),
            pltpu.HBM((rows, channels + LANES), jnp.float32),
            pltpu.HBM((rows, channels), jnp.float32),
            jax.ShapeDtypeStruct((packed.shape[0], channels), jnp.bfloat16),
        ),
        compiler_params=pltpu.CompilerParams(vmem_limit_bytes=VMEM),
        cost_estimate=pl.CostEstimate(
            flops=3 * 4 * rows * channels * channels,
            bytes_accessed=8000000,
            transcendentals=2 * rows * channels,
        ),
    )(jnp.stack([link, core]), lengths, feats, packed, from_link, from_core)


def backward_kernel(
    core_ref, own_ref, other_ref, slope_ref, normed_ref, gain_ref, transposed_ref,
    low_ref, keep_ref, send_ref, sums_ref, paired_ref, sem,
):
    step = pl.program_id(0)
    fetch = pltpu.make_async_copy(transposed_ref, paired_ref, sem)

    @pl.when(step == 0)
    def _():
        fetch.start()

    rows = slope_ref.shape[0]
    first = core_ref[0] == 0
    columns = []
    for link in range(2):
        own = own_ref[0, :, link].astype(jnp.float32).reshape(rows, LANES)
        other = other_ref[:, link].astype(jnp.float32).reshape(rows, LANES)
        columns.append(jnp.where(first, own, other))
        columns.append(jnp.where(first, other, own))
    upstream = jnp.concatenate(columns, axis=1)
    normed = normed_ref[...]
    channels = normed.shape[1]
    grad_act = upstream * slope_ref[:, :channels]
    weighted = grad_act * normed
    gain = parameter(gain_ref[...], 1)
    grad_normed = grad_act * gain
    grad_mean = jnp.sum(grad_normed, axis=1, keepdims=True) * (1.0 / channels)
    cross_mean = jnp.sum(weighted * gain, axis=1, keepdims=True) * (1.0 / channels)
    grad_pre = slope_ref[:, channels : channels + 1] * (grad_normed - grad_mean - normed * cross_mean)
    low_ref[pl.ds(pl.multiple_of(step * rows, 16), rows), :] = grad_pre.astype(jnp.bfloat16)
    sums = jnp.concatenate(
        [
            jnp.sum(grad_pre, axis=0, keepdims=True),
            jnp.sum(weighted, axis=0, keepdims=True),
            jnp.sum(grad_act, axis=0, keepdims=True),
            jnp.zeros((5, channels), jnp.float32),
        ],
        axis=0,
    )

    @pl.when(step == 0)
    def _():
        sums_ref[...] = sums

    @pl.when(step > 0)
    def _():
        sums_ref[...] += sums

    @pl.when(step == pl.num_programs(0) - 1)
    def _():
        fetch.wait()
        depth = paired_ref.shape[0]
        for target_ref, which in ((send_ref, 1 - core_ref[0]), (keep_ref, core_ref[0])):
            places = [pl.ds(pl.multiple_of((2 * link + which) * LANES, LANES), LANES) for link in range(2)]
            columns = jnp.concatenate([low_ref[:, place] for place in places], axis=1)
            product = jnp.dot(paired_ref[...], columns, preferred_element_type=jnp.float32)
            for link in range(2):
                target_ref[link, :depth] = product[:, link * LANES : (link + 1) * LANES]
                target_ref[link, depth:] = sums_ref[:, places[link]]


def backward(core, own, other, slope, normed, gain, transposed):
    steps = 4
    rows, channels = normed.shape
    depth = transposed.shape[0]
    tile = rows // steps
    frames = FRAMES // steps
    half = jax.ShapeDtypeStruct((2, depth + 8, LANES), jnp.float32)
    return pl.pallas_call(
        backward_kernel,
        grid_spec=pltpu.PrefetchScalarGridSpec(
            num_scalar_prefetch=1,
            grid=(steps,),
            in_specs=[
                pl.BlockSpec((1, frames, 2, PAD, LANES), lambda i, core: (core[0], i, 0, 0, 0)),
                pl.BlockSpec((frames, 2, PAD, LANES), lambda i, core: (i, 0, 0, 0)),
                pl.BlockSpec((tile, channels + LANES), lambda i, core: (i, 0)),
                pl.BlockSpec((tile, channels), lambda i, core: (i, 0)),
                pl.BlockSpec((16, channels), lambda i, core: (depth // 16, 0)),
                pl.BlockSpec(memory_space=pl.ANY),
            ],
            out_specs=(
                pl.BlockSpec((rows, channels), lambda i, core: (0, 0)),
                pl.BlockSpec(half.shape, lambda i, core: (0, 0, 0)),
                pl.BlockSpec(half.shape, lambda i, core: (0, 0, 0)),
            ),
            scratch_shapes=[
                pltpu.VMEM((8, channels), jnp.float32),
                pltpu.VMEM((depth, rows), jnp.bfloat16),
                pltpu.SemaphoreType.DMA,
            ],
        ),
        out_shape=(jax.ShapeDtypeStruct((rows, channels), jnp.bfloat16), half, half),
        compiler_params=pltpu.CompilerParams(vmem_limit_bytes=48 * MIB),
        cost_estimate=pl.CostEstimate(
            flops=2 * rows * depth * channels, bytes_accessed=9000000, transcendentals=0
        ),
    )(core.reshape(1), own, other, slope, normed, gain, transposed)


def input_kernel(core_ref, low_ref, weight_ref, keep_ref, send_ref):
    low = low_ref[...]
    for target_ref, which in ((send_ref, 1 - core_ref[0]), (keep_ref, core_ref[0])):
        for tap in range(2):
            rows = [
                weight_ref[pl.ds(pl.multiple_of((4 * tap + 2 * link + which) * LANES, LANES), LANES), :]
                for link in range(2)
            ]
            product = lax.dot_general(
                low, jnp.concatenate(rows, axis=0), (((1,), (1,)), ((), ())),
                preferred_element_type=jnp.float32,
            ).astype(jnp.bfloat16)
            for link in range(2):
                target_ref[link, tap] = product[:, link * LANES : (link + 1) * LANES]


def input_gradient(core, low, weight):
    rows = low.shape[0]
    half = jax.ShapeDtypeStruct((2, 2, rows, LANES), jnp.bfloat16)
    return pl.pallas_call(
        input_kernel,
        out_shape=(half, half),
        in_specs=[
            pl.BlockSpec(memory_space=pltpu.SMEM),
            pl.BlockSpec(memory_space=pltpu.VMEM),
            pl.BlockSpec(memory_space=pltpu.VMEM),
        ],
        out_specs=(pl.BlockSpec(memory_space=pltpu.VMEM),) * 2,
        compiler_params=pltpu.CompilerParams(vmem_limit_bytes=VMEM),
        cost_estimate=pl.CostEstimate(
            flops=4 * rows * weight.shape[1] * weight.shape[1],
            bytes_accessed=3500000,
            transcendentals=0,
        ),
    )(core.reshape(1), low, weight)


def chip_kernel(keep_ref, other_ref, weight_ref, vector_ref):
    total = keep_ref[0] + other_ref[0]
    depth = total.shape[0] - 8
    weight_ref[:, 0] = total[:depth].reshape(DP, depth // DP, LANES).astype(jnp.bfloat16)
    vector_ref[0] = total[depth:]


def chip_total(keep, other):
    depth = keep.shape[1] - 8
    return pl.pallas_call(
        chip_kernel,
        grid=(2,),
        out_shape=(
            jax.ShapeDtypeStruct((DP, 2, depth // DP, LANES), jnp.bfloat16),
            jax.ShapeDtypeStruct((2, 8, LANES), jnp.float32),
        ),
        in_specs=[pl.BlockSpec((1, depth + 8, LANES), lambda i: (i, 0, 0))] * 2,
        out_specs=(
            pl.BlockSpec((DP, 1, depth // DP, LANES), lambda i: (0, i, 0, 0)),
            pl.BlockSpec((1, 8, LANES), lambda i: (i, 0, 0)),
        ),
        compiler_params=pltpu.CompilerParams(vmem_limit_bytes=VMEM),
        cost_estimate=pl.CostEstimate(
            flops=2 * depth * LANES, bytes_accessed=2700000, transcendentals=0
        ),
    )(keep, other)


def route(grad_rows, seg_owner, seg_slot):
    outgoing = lay_out(grad_rows, seg_owner, seg_slot)
    spread = lax.all_to_all(outgoing, "dp", split_axis=0, concat_axis=0, tiled=True)
    sorted_pieces = permute_pieces(spread).reshape(2 * DP, PAD, LANES)
    arrived = lax.all_to_all(
        sorted_pieces, ("dp", "l"), split_axis=0, concat_axis=0, tiled=True
    ).reshape(2, FRAMES, 2, PAD, LANES)
    return arrived, sorted_pieces


def pack_parameters(conv_weight, vectors):
    high = lax.reduce_precision(vectors, 8, 7)
    middle = lax.reduce_precision(vectors - high, 8, 7)
    terms = jnp.concatenate([high, middle, vectors - high - middle]).astype(jnp.bfloat16)
    return jnp.concatenate([conv_weight, jnp.pad(terms, ((0, 7), (0, 0)))], axis=0)


def on_device(
    feats, conv_weight, conv_bias, norm_gain, norm_shift, lengths, grad_rows, seg_owner, seg_slot
):
    link, core = lax.axis_index("l"), lax.axis_index("c")
    channels = 4 * LANES

    own, sorted_pieces = route(grad_rows, seg_owner, seg_slot)

    packed = pack_parameters(conv_weight, jnp.stack([conv_bias, norm_gain, norm_shift]))
    by_group = feats.reshape(SLOTS, 2, 2, 2 * FRAMES, LANES).transpose(1, 2, 0, 3, 4)
    by_group = by_group.reshape(2, 2, SLOTS * 2 * FRAMES, LANES)
    away = pick(by_group, 1 - link, 0)
    from_link = swap(jnp.concatenate([away.reshape(-1, LANES), packed]), "l")
    from_link, _ = lax.optimization_barrier((from_link, sorted_pieces))
    rows = SLOTS * 2 * FRAMES
    beside = jnp.stack(
        [
            jnp.concatenate([pick(pick(by_group, link, 0), 1 - core, 0), packed]),
            jnp.concatenate(
                [
                    lax.dynamic_slice_in_dim(from_link, (1 - core) * rows, rows),
                    from_link[2 * rows :],
                ]
            ),
        ]
    )
    from_core = swap(beside, "c")
    transposed, slope, normed, weight = forward(
        link, core, lengths, feats.reshape(SLOTS, 4, 2 * FRAMES, LANES), packed, from_link, from_core
    )

    leaving, _ = lax.optimization_barrier((pick(own, 1 - core, 0), normed))
    other = swap(leaving, "c")

    low, keep, send = backward(
        core, own, other, slope, normed, weight, transposed
    )
    chip_weight, chip_vector = chip_total(keep, swap(send, "c"))

    scale = 1.0 / math.sqrt(DP * SLOTS * BLOCK)
    group_vector = pick(chip_vector, link, 0) + swap(pick(chip_vector, 1 - link, 0), "l")
    terms = lax.all_to_all(
        chip_weight.reshape(2 * DP, 16, LANES), ("dp", "l"), split_axis=0, concat_axis=0, tiled=True
    )
    total = (jnp.sum(terms.astype(jnp.float32), axis=0) * scale).astype(jnp.bfloat16)
    high = lax.reduce_precision(group_vector[:3], 8, 7)
    rest = group_vector[:3] - high
    pair = jnp.concatenate([high, rest]).astype(jnp.bfloat16)
    announce = jnp.concatenate([total, pair, jnp.zeros((2, LANES), jnp.bfloat16)], axis=0)
    heard = lax.all_to_all(
        jnp.broadcast_to(announce, (DP, PAD, LANES)), "dp", split_axis=0, concat_axis=0, tiled=True
    )
    weight_out = heard[:, :16].reshape(2 * channels, LANES).astype(jnp.float32)
    sums = jnp.sum(heard[:, 16:22].astype(jnp.float32), axis=0)
    vector_out = (sums[:3] + sums[3:]) * scale

    own_rows, leaving_rows = input_gradient(core, low, weight)
    chip_rows = jnp.stack([own_rows, swap(leaving_rows, "c")])
    here = pick(chip_rows, link, 1)
    there = swap(pick(chip_rows, 1 - link, 1), "l")
    groups = []
    for part in (0, 1):
        rows = jnp.where(link == part, here, there)
        groups.extend(ordered(core, rows[0], rows[1]))
    grad_feats = (
        jnp.stack(groups)
        .reshape(4, 2, FRAMES, PAD, LANES)[:, :, :, :SLOTS]
        .transpose(3, 0, 2, 1, 4)
        .reshape(feats.shape)
    )
    return (grad_feats, weight_out, vector_out[0], vector_out[1], vector_out[2])


def solution(mesh):
    grid = Mesh(mesh.devices.reshape(DP, 2, 2), ("dp", "l", "c"))
    mp = ("l", "c")
    placed = (
        P("dp", mp),
        P(None, mp),
        P(mp),
        P(mp),
        P(mp),
        P("dp"),
        P("dp", mp),
        P("dp"),
        P("dp"),
    )
    return jax.shard_map(
        on_device,
        mesh=grid,
        in_specs=placed,
        out_specs=(P("dp", mp), P(None, mp), P(mp), P(mp), P(mp)),
        check_vma=False,
    )
```

```python
import math

import jax
import jax.numpy as jnp
import numpy as np
from jax import lax
from jax.experimental import pallas as pl
from jax.experimental.pallas import tpu as pltpu
from jax.sharding import Mesh, PartitionSpec as P

BLOCK = 128
BPU = 7
SLOTS = 21
PAD = 24
DP = 64
LANES = 128
STEPS = 2
FRAMES = 32

MIB = 1024 * 1024
VMEM = 28 * MIB
ALL_VMEM = 60 * MIB

EPSILON = 1e-05
INV_ROOT_TWO = 0.7071067811865476
INV_ROOT_TAU = 0.3989422804014327


def gelu_slope(value):
    return (
        0.5 * (1.0 + lax.erf(value * INV_ROOT_TWO))
        + value * jnp.exp(-0.5 * value * value) * INV_ROOT_TAU
    )


def swap(value, axis):
    return lax.ppermute(value, axis, [(0, 1), (1, 0)])


def pick(array, index, axis):
    return lax.dynamic_index_in_dim(array, index, axis, keepdims=False)


def ordered(flag, mine, other):
    return jnp.where(flag == 0, mine, other), jnp.where(flag == 0, other, mine)


def lay_out_kernel(
    rows_ref, owner_ref, slot_ref, out_ref, held_ref, owners_ref, slots_ref, wide_ref, sems
):
    copies = [
        pltpu.make_async_copy(rows_ref, held_ref, sems.at[0]),
        pltpu.make_async_copy(owner_ref, owners_ref, sems.at[1]),
        pltpu.make_async_copy(slot_ref, slots_ref, sems.at[2]),
    ]
    for copy in copies:
        copy.start()
    wide_ref[(SLOTS + 2) * BLOCK :] = jnp.zeros((BLOCK, LANES), jnp.float32)
    lane = lax.broadcasted_iota(jnp.int32, (1, LANES), 1)
    for place, label_ref in enumerate((owners_ref, slots_ref)):
        copies[1 + place].wait()
        label = jnp.zeros((1, LANES), jnp.int32)
        for block in range(SLOTS):
            label = jnp.where(lane == block, label_ref[block], label)
        start = (SLOTS + place) * BLOCK
        wide_ref[start : start + BLOCK] = jnp.broadcast_to(
            label.astype(jnp.float32), (BLOCK, LANES)
        )
    copies[0].wait()
    wide_ref[: SLOTS * BLOCK] = held_ref[...].astype(jnp.float32)
    for half in range(2):
        for frame in range(DP):
            column = wide_ref[pl.ds(half * DP + frame, PAD, stride=BLOCK), :]
            out_ref[frame, half] = column.astype(jnp.bfloat16)


def lay_out(grad_rows, seg_owner, seg_slot):
    return pl.pallas_call(
        lay_out_kernel,
        out_shape=jax.ShapeDtypeStruct((DP, 2, PAD, LANES), jnp.bfloat16),
        in_specs=[pl.BlockSpec(memory_space=pl.ANY)] * 3,
        scratch_shapes=[
            pltpu.VMEM((SLOTS * BLOCK, LANES), jnp.bfloat16),
            pltpu.SMEM((SLOTS,), jnp.int32),
            pltpu.SMEM((SLOTS,), jnp.int32),
            pltpu.VMEM((PAD * BLOCK, LANES), jnp.float32),
            pltpu.SemaphoreType.DMA((3,)),
        ],
        compiler_params=pltpu.CompilerParams(vmem_limit_bytes=ALL_VMEM),
        cost_estimate=pl.CostEstimate(flops=0, bytes_accessed=1500000, transcendentals=0),
    )(grad_rows, seg_owner, seg_slot)


def permute_kernel(lane_ref, spread_ref, out_ref, rows_ref, labels_ref, target_ref):
    step = pl.program_id(0)
    owners = out_ref.shape[0]
    tile = owners * PAD
    width = DP * PAD

    @pl.when(step == 0)
    def _():
        for half in range(2):
            values = spread_ref[:, half].astype(jnp.float32).reshape(width, LANES)
            rows_ref[:, half * LANES : (half + 1) * LANES] = values.astype(jnp.bfloat16)
        labels_ref[...] = spread_ref[:, 0, PAD - 8 :].astype(jnp.float32).reshape(DP * 8, LANES)
        block = lane_ref[0:1, :]
        source = lane_ref[1:2, :]
        repeat = jnp.where(
            lax.broadcasted_iota(jnp.int32, (LANES, width), 0) == block, 1.0, 0.0
        ).astype(jnp.bfloat16)
        own_row = lax.broadcasted_iota(jnp.int32, (DP, width), 0) == source
        found = []
        for row in (SLOTS, SLOTS + 1):
            label = labels_ref[pl.ds(row - (PAD - 8), DP, stride=8), :].astype(jnp.bfloat16)
            spun = jnp.dot(label, repeat, preferred_element_type=jnp.float32)
            found.append(jnp.sum(jnp.where(own_row, spun, 0.0), axis=0, keepdims=True))
        target = (found[0] * PAD + found[1]).astype(jnp.int32)
        target_ref[...] = jnp.where(block < SLOTS, target, -1)

    wanted = step * tile + lax.broadcasted_iota(jnp.int32, (tile, DP * PAD), 0)
    choose = jnp.where(target_ref[...] == wanted, 1.0, 0.0).astype(jnp.bfloat16)
    moved = jnp.dot(choose, rows_ref[...], preferred_element_type=jnp.float32)
    for half in range(2):
        values = moved[:, half * LANES : (half + 1) * LANES].reshape(owners, PAD, LANES)
        out_ref[:, half] = values.astype(jnp.bfloat16)


def permute_pieces(spread):
    steps = 2
    width = DP * PAD
    lanes = np.arange(width, dtype=np.int32)
    places = np.concatenate([np.stack([lanes % PAD, lanes // PAD]), np.zeros((6, width), np.int32)])
    return pl.pallas_call(
        permute_kernel,
        grid=(steps,),
        out_shape=jax.ShapeDtypeStruct(spread.shape, jnp.bfloat16),
        in_specs=[
            pl.BlockSpec((8, width), lambda i: (0, 0)),
            pl.BlockSpec(spread.shape, lambda i: (0, 0, 0, 0)),
        ],
        out_specs=pl.BlockSpec((DP // steps, 2, PAD, LANES), lambda i: (i, 0, 0, 0)),
        scratch_shapes=[
            pltpu.VMEM((width, 2 * LANES), jnp.bfloat16),
            pltpu.VMEM((DP * 8, LANES), jnp.float32),
            pltpu.VMEM((1, width), jnp.int32),
        ],
        compiler_params=pltpu.CompilerParams(vmem_limit_bytes=VMEM),
        cost_estimate=pl.CostEstimate(
            flops=4 * 2 * width * width * 2 * LANES, bytes_accessed=1600000, transcendentals=0
        ),
    )(places, spread)


def parameter(terms, which):
    terms = terms.astype(jnp.float32)
    return sum(terms[3 * part + which : 3 * part + which + 1] for part in range(3))


def forward_kernel(
    place_ref, lengths_ref, feats_ref, packed_ref, link_ref, beside_ref,
    transposed_ref, slope_ref, normed_ref, weight_ref, rows_ref, wide_ref,
):
    step = pl.program_id(0)
    link, core = place_ref[0], place_ref[1]
    blocks = SLOTS * 2 * FRAMES
    rows, channels = normed_ref.shape
    frames = rows // PAD

    @pl.when(step == 0)
    def _():
        sources = (
            (link * 2 + core, feats_ref[:, 0].astype(jnp.float32).reshape(blocks, LANES), packed_ref[...]),
            (
                (1 - link) * 2 + core,
                link_ref[pl.ds(pl.multiple_of(core * blocks, 16), blocks), :].astype(jnp.float32),
                link_ref[2 * blocks :],
            ),
            (link * 2 + 1 - core, beside_ref[0, :blocks].astype(jnp.float32), beside_ref[0, blocks:]),
            (
                (1 - link) * 2 + 1 - core,
                beside_ref[1, :blocks].astype(jnp.float32),
                beside_ref[1, blocks:],
            ),
        )
        for place, value, weight in sources:
            rows_ref[place, :blocks] = value
            weight_ref[:, pl.ds(pl.multiple_of(place * LANES, LANES), LANES)] = weight
        rows_ref[:, blocks:] = jnp.zeros((4, (PAD - SLOTS) * 2 * FRAMES, LANES), jnp.float32)

    for frame in range(frames):
        for tap in range(2):
            for piece in range(4):
                start = 2 * (step * frames + frame) + tap
                column = tap * channels + piece * LANES
                wide_ref[frame * PAD : (frame + 1) * PAD, column : column + LANES] = rows_ref[
                    piece, pl.ds(start, PAD, stride=2 * FRAMES), :
                ]
    paired = wide_ref[...].astype(jnp.bfloat16)
    transposed_ref[...] = paired.T
    terms = weight_ref[2 * channels :]
    preact = jnp.dot(paired, weight_ref[: 2 * channels], preferred_element_type=jnp.float32)
    preact = preact + parameter(terms, 0)
    centred = preact - jnp.sum(preact, axis=1, keepdims=True) * (1.0 / channels)
    spread = jnp.sum(centred * centred, axis=1, keepdims=True) * (1.0 / channels)
    inv_spread = lax.rsqrt(spread + EPSILON)
    normed = centred * inv_spread
    slope = gelu_slope(normed * parameter(terms, 1) + parameter(terms, 2))
    slot = lax.broadcasted_iota(jnp.int32, (PAD, 1), 0)
    limit = jnp.zeros((PAD, 1), jnp.int32)
    for index in range(SLOTS):
        valid = lax.div(lengths_ref[index // BPU] - 400, 320) + 1
        here = valid - (index % BPU) * BLOCK - (link * 2 + core) * FRAMES
        limit = jnp.where(slot == index, here, limit)
    limits = jnp.concatenate([limit - frame for frame in range(frames)], axis=0)
    slope_ref[:, :channels] = jnp.where(limits > step * frames, slope, 0.0)
    slope_ref[:, channels:] = jnp.broadcast_to(inv_spread, (rows, LANES))
    normed_ref[...] = normed


def forward(link, core, lengths, feats, packed, from_link, from_core):
    steps = 2
    rows = FRAMES * PAD
    channels = 4 * LANES
    tile = rows // steps
    return pl.pallas_call(
        forward_kernel,
        grid_spec=pltpu.PrefetchScalarGridSpec(
            num_scalar_prefetch=2,
            grid=(steps,),
            in_specs=[
                pl.BlockSpec(
                    (SLOTS, 1, 2 * FRAMES, LANES),
                    lambda i, place, _: (0, 2 * place[0] + place[1], 0, 0),
                ),
                pl.BlockSpec(packed.shape, lambda i, place, _: (0, 0)),
                pl.BlockSpec(from_link.shape, lambda i, place, _: (0, 0)),
                pl.BlockSpec(from_core.shape, lambda i, place, _: (0, 0, 0)),
            ],
            out_specs=(
                pl.BlockSpec((2 * channels, tile), lambda i, place, _: (0, i)),
                pl.BlockSpec((tile, channels + LANES), lambda i, place, _: (i, 0)),
                pl.BlockSpec((tile, channels), lambda i, place, _: (i, 0)),
                pl.BlockSpec((packed.shape[0], channels), lambda i, place, _: (0, 0)),
            ),
            scratch_shapes=[
                pltpu.VMEM((4, PAD * 2 * FRAMES, LANES), jnp.float32),
                pltpu.VMEM((tile, 2 * channels), jnp.float32),
            ],
        ),
        out_shape=(
            pltpu.HBM((2 * channels, rows), jnp.bfloat16),
            pltpu.HBM((rows, channels + LANES), jnp.float32),
            pltpu.HBM((rows, channels), jnp.float32),
            jax.ShapeDtypeStruct((packed.shape[0], channels), jnp.bfloat16),
        ),
        compiler_params=pltpu.CompilerParams(vmem_limit_bytes=VMEM),
        cost_estimate=pl.CostEstimate(
            flops=3 * 4 * rows * channels * channels,
            bytes_accessed=8000000,
            transcendentals=2 * rows * channels,
        ),
    )(jnp.stack([link, core]), lengths, feats, packed, from_link, from_core)


def backward_kernel(
    core_ref, own_ref, other_ref, slope_hbm, normed_hbm, gain_ref, transposed_ref,
    low_ref, keep_ref, send_ref, sums_ref, paired_ref, slope_all, normed_all, sems,
):
    step = pl.program_id(0)
    rows = normed_all.shape[0] // STEPS
    depth = paired_ref.shape[0]
    share = depth // (2 * STEPS)
    fetches = [
        pltpu.make_async_copy(
            transposed_ref.at[pl.ds(part * share, share), :],
            paired_ref.at[pl.ds(part * share, share), :],
            sems.at[2 * STEPS + part],
        )
        for part in range(2 * STEPS)
    ]

    def chunk(source, target, place, sem):
        part = pl.ds(place * rows, rows)
        return pltpu.make_async_copy(source.at[part, :], target.at[part, :], sems.at[sem])

    @pl.when(step == 0)
    def _():
        for place in range(STEPS):
            chunk(slope_hbm, slope_all, place, 2 * place).start()
            chunk(normed_hbm, normed_all, place, 2 * place + 1).start()
        for fetch in fetches:
            fetch.start()

    here = pl.ds(pl.multiple_of(step * rows, 16), rows)
    for place in range(STEPS):

        @pl.when(step == place)
        def _():
            chunk(slope_hbm, slope_all, place, 2 * place).wait()
            chunk(normed_hbm, normed_all, place, 2 * place + 1).wait()

    first = core_ref[0] == 0
    columns = []
    for link in range(2):
        own = own_ref[0, :, link].astype(jnp.float32).reshape(rows, LANES)
        other = other_ref[:, link].astype(jnp.float32).reshape(rows, LANES)
        columns.append(jnp.where(first, own, other))
        columns.append(jnp.where(first, other, own))
    upstream = jnp.concatenate(columns, axis=1)
    normed = normed_all[here, :]
    channels = normed.shape[1]
    grad_act = upstream * slope_all[here, :channels]
    weighted = grad_act * normed
    gain = parameter(gain_ref[...], 1)
    grad_normed = grad_act * gain
    grad_mean = jnp.sum(grad_normed, axis=1, keepdims=True) * (1.0 / channels)
    cross_mean = jnp.sum(weighted * gain, axis=1, keepdims=True) * (1.0 / channels)
    grad_pre = slope_all[here, channels : channels + 1] * (grad_normed - grad_mean - normed * cross_mean)
    low_ref[here, :] = grad_pre.astype(jnp.bfloat16)
    sums = jnp.concatenate(
        [
            jnp.sum(grad_pre, axis=0, keepdims=True),
            jnp.sum(weighted, axis=0, keepdims=True),
            jnp.sum(grad_act, axis=0, keepdims=True),
            jnp.zeros((5, channels), jnp.float32),
        ],
        axis=0,
    )

    @pl.when(step == 0)
    def _():
        sums_ref[...] = sums

    @pl.when(step > 0)
    def _():
        sums_ref[...] += sums

    @pl.when(step == pl.num_programs(0) - 1)
    def _():
        for fetch in fetches:
            fetch.wait()
        for target_ref, which in ((send_ref, 1 - core_ref[0]), (keep_ref, core_ref[0])):
            places = [pl.ds(pl.multiple_of((2 * link + which) * LANES, LANES), LANES) for link in range(2)]
            columns = jnp.concatenate([low_ref[:, place] for place in places], axis=1)
            product = jnp.dot(paired_ref[...], columns, preferred_element_type=jnp.float32)
            for link in range(2):
                part = product[:, link * LANES : (link + 1) * LANES]
                target_ref[link, :depth] = part.astype(target_ref.dtype)
        for link in range(2):
            kept = pl.ds(pl.multiple_of((2 * link + core_ref[0]) * LANES, LANES), LANES)
            keep_ref[link, depth:] = sums_ref[:, kept]
            sent = pl.ds(pl.multiple_of((2 * link + 1 - core_ref[0]) * LANES, LANES), LANES)
            value = sums_ref[:, sent]
            high = value.astype(jnp.bfloat16).astype(jnp.float32)
            send_ref[link, depth:] = jnp.concatenate([high, value - high], axis=0).astype(
                jnp.bfloat16
            )


def backward(core, own, other, slope, normed, gain, transposed):
    rows, channels = normed.shape
    depth = transposed.shape[0]
    frames = FRAMES // STEPS
    half = jax.ShapeDtypeStruct((2, depth + 8, LANES), jnp.float32)
    leaving = jax.ShapeDtypeStruct((2, depth + 16, LANES), jnp.bfloat16)
    return pl.pallas_call(
        backward_kernel,
        grid_spec=pltpu.PrefetchScalarGridSpec(
            num_scalar_prefetch=1,
            grid=(STEPS,),
            in_specs=[
                pl.BlockSpec((1, frames, 2, PAD, LANES), lambda i, core: (core[0], i, 0, 0, 0)),
                pl.BlockSpec((frames, 2, PAD, LANES), lambda i, core: (i, 0, 0, 0)),
                pl.BlockSpec(memory_space=pl.ANY),
                pl.BlockSpec(memory_space=pl.ANY),
                pl.BlockSpec((16, channels), lambda i, core: (depth // 16, 0)),
                pl.BlockSpec(memory_space=pl.ANY),
            ],
            out_specs=(
                pl.BlockSpec((rows, channels), lambda i, core: (0, 0)),
                pl.BlockSpec(half.shape, lambda i, core: (0, 0, 0)),
                pl.BlockSpec(leaving.shape, lambda i, core: (0, 0, 0)),
            ),
            scratch_shapes=[
                pltpu.VMEM((8, channels), jnp.float32),
                pltpu.VMEM((depth, rows), jnp.bfloat16),
                pltpu.VMEM((rows, channels + LANES), jnp.float32),
                pltpu.VMEM((rows, channels), jnp.float32),
                pltpu.SemaphoreType.DMA((4 * STEPS,)),
            ],
        ),
        out_shape=(jax.ShapeDtypeStruct((rows, channels), jnp.bfloat16), half, leaving),
        compiler_params=pltpu.CompilerParams(vmem_limit_bytes=48 * MIB),
        cost_estimate=pl.CostEstimate(
            flops=2 * rows * depth * channels, bytes_accessed=9000000, transcendentals=0
        ),
    )(core.reshape(1), own, other, slope, normed, gain, transposed)


def input_kernel(core_ref, low_ref, weight_ref, keep_ref, send_ref):
    low = low_ref[...]
    for target_ref, which in ((send_ref, 1 - core_ref[0]), (keep_ref, core_ref[0])):
        for tap in range(2):
            rows = [
                weight_ref[pl.ds(pl.multiple_of((4 * tap + 2 * link + which) * LANES, LANES), LANES), :]
                for link in range(2)
            ]
            product = lax.dot_general(
                low, jnp.concatenate(rows, axis=0), (((1,), (1,)), ((), ())),
                preferred_element_type=jnp.float32,
            ).astype(jnp.bfloat16)
            for link in range(2):
                target_ref[link, tap] = product[:, link * LANES : (link + 1) * LANES]


def input_gradient(core, low, weight):
    rows = low.shape[0]
    half = jax.ShapeDtypeStruct((2, 2, rows, LANES), jnp.bfloat16)
    return pl.pallas_call(
        input_kernel,
        out_shape=(half, half),
        in_specs=[
            pl.BlockSpec(memory_space=pltpu.SMEM),
            pl.BlockSpec(memory_space=pltpu.VMEM),
            pl.BlockSpec(memory_space=pltpu.VMEM),
        ],
        out_specs=(pl.BlockSpec(memory_space=pltpu.VMEM),) * 2,
        compiler_params=pltpu.CompilerParams(vmem_limit_bytes=VMEM),
        cost_estimate=pl.CostEstimate(
            flops=4 * rows * weight.shape[1] * weight.shape[1],
            bytes_accessed=3500000,
            transcendentals=0,
        ),
    )(core.reshape(1), low, weight)


def chip_kernel(keep_ref, other_ref, weight_ref, vector_ref):
    depth = keep_ref.shape[1] - 8
    total = keep_ref[0, :depth] + other_ref[0, :depth].astype(jnp.float32)
    weight_ref[:, 0] = total.reshape(DP, depth // DP, LANES).astype(jnp.bfloat16)
    terms = other_ref[0, depth:].astype(jnp.float32)
    vector_ref[0] = keep_ref[0, depth:] + (terms[:8] + terms[8:])


def chip_total(keep, other):
    depth = keep.shape[1] - 8
    return pl.pallas_call(
        chip_kernel,
        grid=(2,),
        out_shape=(
            jax.ShapeDtypeStruct((DP, 2, depth // DP, LANES), jnp.bfloat16),
            jax.ShapeDtypeStruct((2, 8, LANES), jnp.float32),
        ),
        in_specs=[
            pl.BlockSpec((1, depth + 8, LANES), lambda i: (i, 0, 0)),
            pl.BlockSpec((1, depth + 16, LANES), lambda i: (i, 0, 0)),
        ],
        out_specs=(
            pl.BlockSpec((DP, 1, depth // DP, LANES), lambda i: (0, i, 0, 0)),
            pl.BlockSpec((1, 8, LANES), lambda i: (i, 0, 0)),
        ),
        compiler_params=pltpu.CompilerParams(vmem_limit_bytes=VMEM),
        cost_estimate=pl.CostEstimate(
            flops=2 * depth * LANES, bytes_accessed=2700000, transcendentals=0
        ),
    )(keep, other)


def route(grad_rows, seg_owner, seg_slot):
    outgoing = lay_out(grad_rows, seg_owner, seg_slot)
    spread = lax.all_to_all(outgoing, "dp", split_axis=0, concat_axis=0, tiled=True)
    sorted_pieces = permute_pieces(spread).reshape(2 * DP, PAD, LANES)
    arrived = lax.all_to_all(
        sorted_pieces, ("dp", "l"), split_axis=0, concat_axis=0, tiled=True
    ).reshape(2, FRAMES, 2, PAD, LANES)
    return arrived, sorted_pieces


def pack_parameters(conv_weight, vectors):
    high = lax.reduce_precision(vectors, 8, 7)
    middle = lax.reduce_precision(vectors - high, 8, 7)
    terms = jnp.concatenate([high, middle, vectors - high - middle]).astype(jnp.bfloat16)
    return jnp.concatenate([conv_weight, jnp.pad(terms, ((0, 7), (0, 0)))], axis=0)


def on_device(
    feats, conv_weight, conv_bias, norm_gain, norm_shift, lengths, grad_rows, seg_owner, seg_slot
):
    link, core = lax.axis_index("l"), lax.axis_index("c")
    channels = 4 * LANES

    own, sorted_pieces = route(grad_rows, seg_owner, seg_slot)

    packed = pack_parameters(conv_weight, jnp.stack([conv_bias, norm_gain, norm_shift]))
    by_group = feats.reshape(SLOTS, 2, 2, 2 * FRAMES, LANES).transpose(1, 2, 0, 3, 4)
    by_group = by_group.reshape(2, 2, SLOTS * 2 * FRAMES, LANES)
    away = pick(by_group, 1 - link, 0)
    from_link = swap(jnp.concatenate([away.reshape(-1, LANES), packed]), "l")
    from_link, _ = lax.optimization_barrier((from_link, sorted_pieces))
    rows = SLOTS * 2 * FRAMES
    beside = jnp.stack(
        [
            jnp.concatenate([pick(pick(by_group, link, 0), 1 - core, 0), packed]),
            jnp.concatenate(
                [
                    lax.dynamic_slice_in_dim(from_link, (1 - core) * rows, rows),
                    from_link[2 * rows :],
                ]
            ),
        ]
    )
    from_core = swap(beside, "c")
    transposed, slope, normed, weight = forward(
        link, core, lengths, feats.reshape(SLOTS, 4, 2 * FRAMES, LANES), packed, from_link, from_core
    )

    leaving, _ = lax.optimization_barrier((pick(own, 1 - core, 0), normed))
    other = swap(leaving, "c")

    low, keep, send = backward(
        core, own, other, slope, normed, weight, transposed
    )
    chip_weight, chip_vector = chip_total(keep, swap(send, "c"))

    scale = 1.0 / math.sqrt(DP * SLOTS * BLOCK)
    group_vector = pick(chip_vector, link, 0) + swap(pick(chip_vector, 1 - link, 0), "l")
    terms = lax.all_to_all(
        chip_weight.reshape(2 * DP, 16, LANES), ("dp", "l"), split_axis=0, concat_axis=0, tiled=True
    )
    total = (jnp.sum(terms.astype(jnp.float32), axis=0) * scale).astype(jnp.bfloat16)
    high = lax.reduce_precision(group_vector[:3], 8, 7)
    rest = group_vector[:3] - high
    pair = jnp.concatenate([high, rest]).astype(jnp.bfloat16)
    announce = jnp.concatenate([total, pair, jnp.zeros((2, LANES), jnp.bfloat16)], axis=0)
    heard = lax.all_to_all(
        jnp.broadcast_to(announce, (DP, PAD, LANES)), "dp", split_axis=0, concat_axis=0, tiled=True
    )
    weight_out = heard[:, :16].reshape(2 * channels, LANES).astype(jnp.float32)
    sums = jnp.sum(heard[:, 16:22].astype(jnp.float32), axis=0)
    vector_out = (sums[:3] + sums[3:]) * scale

    own_rows, leaving_rows = input_gradient(core, low, weight)
    chip_rows = jnp.stack([own_rows, swap(leaving_rows, "c")])
    here = pick(chip_rows, link, 1)
    there = swap(pick(chip_rows, 1 - link, 1), "l")
    groups = []
    for part in (0, 1):
        rows = jnp.where(link == part, here, there)
        groups.extend(ordered(core, rows[0], rows[1]))
    grad_feats = (
        jnp.stack(groups)
        .reshape(4, 2, FRAMES, PAD, LANES)[:, :, :, :SLOTS]
        .transpose(3, 0, 2, 1, 4)
        .reshape(feats.shape)
    )
    return (grad_feats, weight_out, vector_out[0], vector_out[1], vector_out[2])


def solution(mesh):
    grid = Mesh(mesh.devices.reshape(DP, 2, 2), ("dp", "l", "c"))
    mp = ("l", "c")
    placed = (
        P("dp", mp),
        P(None, mp),
        P(mp),
        P(mp),
        P(mp),
        P("dp"),
        P("dp", mp),
        P("dp"),
        P("dp"),
    )
    return jax.shard_map(
        on_device,
        mesh=grid,
        in_specs=placed,
        out_specs=(P("dp", mp), P(None, mp), P(mp), P(mp), P(mp)),
        check_vma=False,
    )
```

```python
import math

import jax
import jax.numpy as jnp
import numpy as np
from jax import lax
from jax.experimental import pallas as pl
from jax.experimental.pallas import tpu as pltpu
from jax.sharding import Mesh, PartitionSpec as P

BLOCK = 128
BPU = 7
SLOTS = 21
PAD = 24
DP = 64
LANES = 128
STEPS = 4
FRAMES = 32

MIB = 1024 * 1024
VMEM = 28 * MIB
BRING = 52 * MIB
ALL_VMEM = 60 * MIB

EPSILON = 1e-05
INV_ROOT_TWO = 0.7071067811865476
INV_ROOT_TAU = 0.3989422804014327


def gelu_slope(value):
    return (
        0.5 * (1.0 + lax.erf(value * INV_ROOT_TWO))
        + value * jnp.exp(-0.5 * value * value) * INV_ROOT_TAU
    )


def swap(value, axis):
    return lax.ppermute(value, axis, [(0, 1), (1, 0)])


def pick(array, index, axis):
    return lax.dynamic_index_in_dim(array, index, axis, keepdims=False)


def ordered(flag, mine, other):
    return jnp.where(flag == 0, mine, other), jnp.where(flag == 0, other, mine)


def lay_out_kernel(
    rows_ref, owner_ref, slot_ref, out_ref, held_ref, owners_ref, slots_ref, wide_ref, sems
):
    copies = [
        pltpu.make_async_copy(rows_ref, held_ref, sems.at[0]),
        pltpu.make_async_copy(owner_ref, owners_ref, sems.at[1]),
        pltpu.make_async_copy(slot_ref, slots_ref, sems.at[2]),
    ]
    for copy in copies:
        copy.start()
    wide_ref[(SLOTS + 2) * BLOCK :] = jnp.zeros((BLOCK, LANES), jnp.float32)
    lane = lax.broadcasted_iota(jnp.int32, (1, LANES), 1)
    for place, label_ref in enumerate((owners_ref, slots_ref)):
        copies[1 + place].wait()
        label = jnp.zeros((1, LANES), jnp.int32)
        for block in range(SLOTS):
            label = jnp.where(lane == block, label_ref[block], label)
        start = (SLOTS + place) * BLOCK
        wide_ref[start : start + BLOCK] = jnp.broadcast_to(
            label.astype(jnp.float32), (BLOCK, LANES)
        )
    copies[0].wait()
    wide_ref[: SLOTS * BLOCK] = held_ref[...].astype(jnp.float32)
    for half in range(2):
        for frame in range(DP):
            column = wide_ref[pl.ds(half * DP + frame, PAD, stride=BLOCK), :]
            out_ref[frame, half] = column.astype(jnp.bfloat16)


def lay_out(grad_rows, seg_owner, seg_slot):
    return pl.pallas_call(
        lay_out_kernel,
        out_shape=jax.ShapeDtypeStruct((DP, 2, PAD, LANES), jnp.bfloat16),
        in_specs=[pl.BlockSpec(memory_space=pl.ANY)] * 3,
        scratch_shapes=[
            pltpu.VMEM((SLOTS * BLOCK, LANES), jnp.bfloat16),
            pltpu.SMEM((SLOTS,), jnp.int32),
            pltpu.SMEM((SLOTS,), jnp.int32),
            pltpu.VMEM((PAD * BLOCK, LANES), jnp.float32),
            pltpu.SemaphoreType.DMA((3,)),
        ],
        compiler_params=pltpu.CompilerParams(vmem_limit_bytes=ALL_VMEM),
        cost_estimate=pl.CostEstimate(flops=0, bytes_accessed=1500000, transcendentals=0),
    )(grad_rows, seg_owner, seg_slot)


def permute_kernel(lane_ref, spread_ref, out_ref, rows_ref, labels_ref, target_ref):
    step = pl.program_id(0)
    owners = out_ref.shape[0]
    tile = owners * PAD
    width = DP * PAD

    @pl.when(step == 0)
    def _():
        for half in range(2):
            values = spread_ref[:, half].astype(jnp.float32).reshape(width, LANES)
            rows_ref[:, half * LANES : (half + 1) * LANES] = values.astype(jnp.bfloat16)
        labels_ref[...] = spread_ref[:, 0, PAD - 8 :].astype(jnp.float32).reshape(DP * 8, LANES)
        block = lane_ref[0:1, :]
        source = lane_ref[1:2, :]
        repeat = jnp.where(
            lax.broadcasted_iota(jnp.int32, (LANES, width), 0) == block, 1.0, 0.0
        ).astype(jnp.bfloat16)
        own_row = lax.broadcasted_iota(jnp.int32, (DP, width), 0) == source
        found = []
        for row in (SLOTS, SLOTS + 1):
            label = labels_ref[pl.ds(row - (PAD - 8), DP, stride=8), :].astype(jnp.bfloat16)
            spun = jnp.dot(label, repeat, preferred_element_type=jnp.float32)
            found.append(jnp.sum(jnp.where(own_row, spun, 0.0), axis=0, keepdims=True))
        target = (found[0] * PAD + found[1]).astype(jnp.int32)
        target_ref[...] = jnp.where(block < SLOTS, target, -1)

    wanted = step * tile + lax.broadcasted_iota(jnp.int32, (tile, DP * PAD), 0)
    choose = jnp.where(target_ref[...] == wanted, 1.0, 0.0).astype(jnp.bfloat16)
    moved = jnp.dot(choose, rows_ref[...], preferred_element_type=jnp.float32)
    for half in range(2):
        values = moved[:, half * LANES : (half + 1) * LANES].reshape(owners, PAD, LANES)
        out_ref[:, half] = values.astype(jnp.bfloat16)


def permute_pieces(spread):
    steps = 2
    width = DP * PAD
    lanes = np.arange(width, dtype=np.int32)
    places = np.concatenate([np.stack([lanes % PAD, lanes // PAD]), np.zeros((6, width), np.int32)])
    return pl.pallas_call(
        permute_kernel,
        grid=(steps,),
        out_shape=jax.ShapeDtypeStruct(spread.shape, jnp.bfloat16),
        in_specs=[
            pl.BlockSpec((8, width), lambda i: (0, 0)),
            pl.BlockSpec(spread.shape, lambda i: (0, 0, 0, 0)),
        ],
        out_specs=pl.BlockSpec((DP // steps, 2, PAD, LANES), lambda i: (i, 0, 0, 0)),
        scratch_shapes=[
            pltpu.VMEM((width, 2 * LANES), jnp.bfloat16),
            pltpu.VMEM((DP * 8, LANES), jnp.float32),
            pltpu.VMEM((1, width), jnp.int32),
        ],
        compiler_params=pltpu.CompilerParams(vmem_limit_bytes=VMEM),
        cost_estimate=pl.CostEstimate(
            flops=4 * 2 * width * width * 2 * LANES, bytes_accessed=1600000, transcendentals=0
        ),
    )(places, spread)


def parameter(terms, which):
    terms = terms.astype(jnp.float32)
    return sum(terms[3 * part + which : 3 * part + which + 1] for part in range(3))


def forward_kernel(
    place_ref, lengths_ref, feats_ref, packed_ref, link_ref, beside_ref,
    transposed_ref, slope_ref, normed_ref, weight_ref, rows_ref, wide_ref,
):
    step = pl.program_id(0)
    link, core = place_ref[0], place_ref[1]
    blocks = SLOTS * 2 * FRAMES
    rows, channels = normed_ref.shape
    frames = rows // PAD

    @pl.when(step == 0)
    def _():
        sources = (
            (link * 2 + core, feats_ref[:, 0].astype(jnp.float32).reshape(blocks, LANES), packed_ref[...]),
            (
                (1 - link) * 2 + core,
                link_ref[pl.ds(pl.multiple_of(core * blocks, 16), blocks), :].astype(jnp.float32),
                link_ref[2 * blocks :],
            ),
            (link * 2 + 1 - core, beside_ref[0, :blocks].astype(jnp.float32), beside_ref[0, blocks:]),
            (
                (1 - link) * 2 + 1 - core,
                beside_ref[1, :blocks].astype(jnp.float32),
                beside_ref[1, blocks:],
            ),
        )
        for place, value, weight in sources:
            rows_ref[place, :blocks] = value
            weight_ref[:, pl.ds(pl.multiple_of(place * LANES, LANES), LANES)] = weight
        rows_ref[:, blocks:] = jnp.zeros((4, (PAD - SLOTS) * 2 * FRAMES, LANES), jnp.float32)

    for frame in range(frames):
        for tap in range(2):
            for piece in range(4):
                start = 2 * (step * frames + frame) + tap
                column = tap * channels + piece * LANES
                wide_ref[frame * PAD : (frame + 1) * PAD, column : column + LANES] = rows_ref[
                    piece, pl.ds(start, PAD, stride=2 * FRAMES), :
                ]
    paired = wide_ref[...].astype(jnp.bfloat16)
    transposed_ref[...] = paired.T
    terms = weight_ref[2 * channels :]
    preact = jnp.dot(paired, weight_ref[: 2 * channels], preferred_element_type=jnp.float32)
    preact = preact + parameter(terms, 0)
    centred = preact - jnp.sum(preact, axis=1, keepdims=True) * (1.0 / channels)
    spread = jnp.sum(centred * centred, axis=1, keepdims=True) * (1.0 / channels)
    inv_spread = lax.rsqrt(spread + EPSILON)
    normed = centred * inv_spread
    slope = gelu_slope(normed * parameter(terms, 1) + parameter(terms, 2))
    slot = lax.broadcasted_iota(jnp.int32, (PAD, 1), 0)
    limit = jnp.zeros((PAD, 1), jnp.int32)
    for index in range(SLOTS):
        valid = lax.div(lengths_ref[index // BPU] - 400, 320) + 1
        here = valid - (index % BPU) * BLOCK - (link * 2 + core) * FRAMES
        limit = jnp.where(slot == index, here, limit)
    limits = jnp.concatenate([limit - frame for frame in range(frames)], axis=0)
    slope_ref[:, :channels] = jnp.where(limits > step * frames, slope, 0.0)
    slope_ref[:, channels:] = jnp.broadcast_to(inv_spread, (rows, LANES))
    normed_ref[...] = normed


def forward(link, core, lengths, feats, packed, from_link, from_core):
    steps = 2
    rows = FRAMES * PAD
    channels = 4 * LANES
    tile = rows // steps
    return pl.pallas_call(
        forward_kernel,
        grid_spec=pltpu.PrefetchScalarGridSpec(
            num_scalar_prefetch=2,
            grid=(steps,),
            in_specs=[
                pl.BlockSpec(
                    (SLOTS, 1, 2 * FRAMES, LANES),
                    lambda i, place, _: (0, 2 * place[0] + place[1], 0, 0),
                ),
                pl.BlockSpec(packed.shape, lambda i, place, _: (0, 0)),
                pl.BlockSpec(from_link.shape, lambda i, place, _: (0, 0)),
                pl.BlockSpec(from_core.shape, lambda i, place, _: (0, 0, 0)),
            ],
            out_specs=(
                pl.BlockSpec((2 * channels, tile), lambda i, place, _: (0, i)),
                pl.BlockSpec((tile, channels + LANES), lambda i, place, _: (i, 0)),
                pl.BlockSpec((tile, channels), lambda i, place, _: (i, 0)),
                pl.BlockSpec((packed.shape[0], channels), lambda i, place, _: (0, 0)),
            ),
            scratch_shapes=[
                pltpu.VMEM((4, PAD * 2 * FRAMES, LANES), jnp.float32),
                pltpu.VMEM((tile, 2 * channels), jnp.float32),
            ],
        ),
        out_shape=(
            pltpu.HBM((2 * channels, rows), jnp.bfloat16),
            pltpu.HBM((rows, channels + LANES), jnp.float32),
            pltpu.HBM((rows, channels), jnp.float32),
            jax.ShapeDtypeStruct((packed.shape[0], channels), jnp.bfloat16),
        ),
        compiler_params=pltpu.CompilerParams(vmem_limit_bytes=VMEM),
        cost_estimate=pl.CostEstimate(
            flops=3 * 4 * rows * channels * channels,
            bytes_accessed=8000000,
            transcendentals=2 * rows * channels,
        ),
    )(jnp.stack([link, core]), lengths, feats, packed, from_link, from_core)


def bring_kernel(slope_hbm, normed_hbm, transposed_hbm, slope_ref, normed_ref, transposed_ref, sems):
    copies = []
    for source, target in (
        (slope_hbm, slope_ref), (normed_hbm, normed_ref), (transposed_hbm, transposed_ref)
    ):
        share = source.shape[0] // 4
        for part in range(4):
            place = pl.ds(part * share, share)
            copies.append(
                pltpu.make_async_copy(source.at[place, :], target.at[place, :], sems.at[len(copies)])
            )
    for copy in copies:
        copy.start()
    for copy in copies:
        copy.wait()


def bring(slope, normed, transposed):
    arrays = (slope, normed, transposed)
    return pl.pallas_call(
        bring_kernel,
        out_shape=tuple(pltpu.VMEM(array.shape, array.dtype) for array in arrays),
        in_specs=[pl.BlockSpec(memory_space=pl.ANY)] * 3,
        out_specs=(pl.BlockSpec(memory_space=pltpu.VMEM),) * 3,
        scratch_shapes=[pltpu.SemaphoreType.DMA((12,))],
        compiler_params=pltpu.CompilerParams(vmem_limit_bytes=BRING),
        cost_estimate=pl.CostEstimate(flops=0, bytes_accessed=10000000, transcendentals=0),
    )(*arrays)


def backward_kernel(
    core_ref, own_ref, other_ref, slope_ref, normed_ref, gain_ref, transposed_ref,
    low_ref, keep_ref, send_ref, sums_ref,
):
    step = pl.program_id(0)
    rows = normed_ref.shape[0]
    here = pl.ds(pl.multiple_of(step * rows, 16), rows)
    first = core_ref[0] == 0
    columns = []
    for link in range(2):
        own = own_ref[0, :, link].astype(jnp.float32).reshape(rows, LANES)
        other = other_ref[:, link].astype(jnp.float32).reshape(rows, LANES)
        columns.append(jnp.where(first, own, other))
        columns.append(jnp.where(first, other, own))
    upstream = jnp.concatenate(columns, axis=1)
    normed = normed_ref[...]
    channels = normed.shape[1]
    grad_act = upstream * slope_ref[:, :channels]
    weighted = grad_act * normed
    gain = parameter(gain_ref[...], 1)
    grad_normed = grad_act * gain
    grad_mean = jnp.sum(grad_normed, axis=1, keepdims=True) * (1.0 / channels)
    cross_mean = jnp.sum(weighted * gain, axis=1, keepdims=True) * (1.0 / channels)
    grad_pre = slope_ref[:, channels : channels + 1] * (grad_normed - grad_mean - normed * cross_mean)
    low_ref[here, :] = grad_pre.astype(jnp.bfloat16)
    sums = jnp.concatenate(
        [
            jnp.sum(grad_pre, axis=0, keepdims=True),
            jnp.sum(weighted, axis=0, keepdims=True),
            jnp.sum(grad_act, axis=0, keepdims=True),
            jnp.zeros((5, channels), jnp.float32),
        ],
        axis=0,
    )

    @pl.when(step == 0)
    def _():
        sums_ref[...] = sums

    @pl.when(step > 0)
    def _():
        sums_ref[...] += sums

    @pl.when(step == pl.num_programs(0) - 1)
    def _():
        depth = transposed_ref.shape[0]
        for target_ref, which in ((send_ref, 1 - core_ref[0]), (keep_ref, core_ref[0])):
            places = [pl.ds(pl.multiple_of((2 * link + which) * LANES, LANES), LANES) for link in range(2)]
            columns = jnp.concatenate([low_ref[:, place] for place in places], axis=1)
            product = jnp.dot(transposed_ref[...], columns, preferred_element_type=jnp.float32)
            for link in range(2):
                part = product[:, link * LANES : (link + 1) * LANES]
                target_ref[link, :depth] = part.astype(target_ref.dtype)
        for link in range(2):
            kept = pl.ds(pl.multiple_of((2 * link + core_ref[0]) * LANES, LANES), LANES)
            keep_ref[link, depth:] = sums_ref[:, kept]
            sent = pl.ds(pl.multiple_of((2 * link + 1 - core_ref[0]) * LANES, LANES), LANES)
            value = sums_ref[:, sent]
            high = value.astype(jnp.bfloat16).astype(jnp.float32)
            send_ref[link, depth:] = jnp.concatenate([high, value - high], axis=0).astype(
                jnp.bfloat16
            )


def backward(core, own, other, slope, normed, gain, transposed):
    rows, channels = normed.shape
    depth = transposed.shape[0]
    frames = FRAMES // STEPS
    half = jax.ShapeDtypeStruct((2, depth + 8, LANES), jnp.float32)
    leaving = jax.ShapeDtypeStruct((2, depth + 16, LANES), jnp.bfloat16)
    return pl.pallas_call(
        backward_kernel,
        grid_spec=pltpu.PrefetchScalarGridSpec(
            num_scalar_prefetch=1,
            grid=(STEPS,),
            in_specs=[
                pl.BlockSpec((1, frames, 2, PAD, LANES), lambda i, core: (core[0], i, 0, 0, 0)),
                pl.BlockSpec((frames, 2, PAD, LANES), lambda i, core: (i, 0, 0, 0)),
                pl.BlockSpec((rows // STEPS, channels + LANES), lambda i, core: (i, 0)),
                pl.BlockSpec((rows // STEPS, channels), lambda i, core: (i, 0)),
                pl.BlockSpec((16, channels), lambda i, core: (depth // 16, 0)),
                pl.BlockSpec((depth, rows), lambda i, core: (0, 0)),
            ],
            out_specs=(
                pl.BlockSpec((rows, channels), lambda i, core: (0, 0)),
                pl.BlockSpec(half.shape, lambda i, core: (0, 0, 0)),
                pl.BlockSpec(leaving.shape, lambda i, core: (0, 0, 0)),
            ),
            scratch_shapes=[pltpu.VMEM((8, channels), jnp.float32)],
        ),
        out_shape=(jax.ShapeDtypeStruct((rows, channels), jnp.bfloat16), half, leaving),
        compiler_params=pltpu.CompilerParams(vmem_limit_bytes=28 * MIB),
        cost_estimate=pl.CostEstimate(
            flops=2 * rows * depth * channels, bytes_accessed=9000000, transcendentals=0
        ),
    )(core.reshape(1), own, other, slope, normed, gain, transposed)


def input_kernel(core_ref, low_ref, weight_ref, keep_ref, send_ref):
    low = low_ref[...]
    for target_ref, which in ((send_ref, 1 - core_ref[0]), (keep_ref, core_ref[0])):
        for tap in range(2):
            rows = [
                weight_ref[pl.ds(pl.multiple_of((4 * tap + 2 * link + which) * LANES, LANES), LANES), :]
                for link in range(2)
            ]
            product = lax.dot_general(
                low, jnp.concatenate(rows, axis=0), (((1,), (1,)), ((), ())),
                preferred_element_type=jnp.float32,
            ).astype(jnp.bfloat16)
            for link in range(2):
                target_ref[link, tap] = product[:, link * LANES : (link + 1) * LANES]


def input_gradient(core, low, weight):
    rows = low.shape[0]
    half = jax.ShapeDtypeStruct((2, 2, rows, LANES), jnp.bfloat16)
    return pl.pallas_call(
        input_kernel,
        out_shape=(half, half),
        in_specs=[
            pl.BlockSpec(memory_space=pltpu.SMEM),
            pl.BlockSpec(memory_space=pltpu.VMEM),
            pl.BlockSpec(memory_space=pltpu.VMEM),
        ],
        out_specs=(pl.BlockSpec(memory_space=pltpu.VMEM),) * 2,
        compiler_params=pltpu.CompilerParams(vmem_limit_bytes=VMEM),
        cost_estimate=pl.CostEstimate(
            flops=4 * rows * weight.shape[1] * weight.shape[1],
            bytes_accessed=3500000,
            transcendentals=0,
        ),
    )(core.reshape(1), low, weight)


def chip_kernel(keep_ref, other_ref, weight_ref, vector_ref):
    depth = keep_ref.shape[1] - 8
    total = keep_ref[0, :depth] + other_ref[0, :depth].astype(jnp.float32)
    weight_ref[:, 0] = total.reshape(DP, depth // DP, LANES).astype(jnp.bfloat16)
    terms = other_ref[0, depth:].astype(jnp.float32)
    vector_ref[0] = keep_ref[0, depth:] + (terms[:8] + terms[8:])


def chip_total(keep, other):
    depth = keep.shape[1] - 8
    return pl.pallas_call(
        chip_kernel,
        grid=(2,),
        out_shape=(
            jax.ShapeDtypeStruct((DP, 2, depth // DP, LANES), jnp.bfloat16),
            jax.ShapeDtypeStruct((2, 8, LANES), jnp.float32),
        ),
        in_specs=[
            pl.BlockSpec((1, depth + 8, LANES), lambda i: (i, 0, 0)),
            pl.BlockSpec((1, depth + 16, LANES), lambda i: (i, 0, 0)),
        ],
        out_specs=(
            pl.BlockSpec((DP, 1, depth // DP, LANES), lambda i: (0, i, 0, 0)),
            pl.BlockSpec((1, 8, LANES), lambda i: (i, 0, 0)),
        ),
        compiler_params=pltpu.CompilerParams(vmem_limit_bytes=VMEM),
        cost_estimate=pl.CostEstimate(
            flops=2 * depth * LANES, bytes_accessed=2700000, transcendentals=0
        ),
    )(keep, other)


def route(grad_rows, seg_owner, seg_slot):
    outgoing = lay_out(grad_rows, seg_owner, seg_slot)
    spread = lax.all_to_all(outgoing, "dp", split_axis=0, concat_axis=0, tiled=True)
    sorted_pieces = permute_pieces(spread).reshape(2 * DP, PAD, LANES)
    arrived = lax.all_to_all(
        sorted_pieces, ("dp", "l"), split_axis=0, concat_axis=0, tiled=True
    ).reshape(2, FRAMES, 2, PAD, LANES)
    return arrived, sorted_pieces


def pack_parameters(conv_weight, vectors):
    high = lax.reduce_precision(vectors, 8, 7)
    middle = lax.reduce_precision(vectors - high, 8, 7)
    terms = jnp.concatenate([high, middle, vectors - high - middle]).astype(jnp.bfloat16)
    return jnp.concatenate([conv_weight, jnp.pad(terms, ((0, 7), (0, 0)))], axis=0)


def on_device(
    feats, conv_weight, conv_bias, norm_gain, norm_shift, lengths, grad_rows, seg_owner, seg_slot
):
    link, core = lax.axis_index("l"), lax.axis_index("c")
    channels = 4 * LANES

    own, sorted_pieces = route(grad_rows, seg_owner, seg_slot)

    packed = pack_parameters(conv_weight, jnp.stack([conv_bias, norm_gain, norm_shift]))
    by_group = feats.reshape(SLOTS, 2, 2, 2 * FRAMES, LANES).transpose(1, 2, 0, 3, 4)
    by_group = by_group.reshape(2, 2, SLOTS * 2 * FRAMES, LANES)
    away = pick(by_group, 1 - link, 0)
    from_link = swap(jnp.concatenate([away.reshape(-1, LANES), packed]), "l")
    from_link, _ = lax.optimization_barrier((from_link, sorted_pieces))
    rows = SLOTS * 2 * FRAMES
    beside = jnp.stack(
        [
            jnp.concatenate([pick(pick(by_group, link, 0), 1 - core, 0), packed]),
            jnp.concatenate(
                [
                    lax.dynamic_slice_in_dim(from_link, (1 - core) * rows, rows),
                    from_link[2 * rows :],
                ]
            ),
        ]
    )
    from_core = swap(beside, "c")
    transposed, slope, normed, weight = forward(
        link, core, lengths, feats.reshape(SLOTS, 4, 2 * FRAMES, LANES), packed, from_link, from_core
    )

    leaving, slope, normed, transposed = lax.optimization_barrier(
        (pick(own, 1 - core, 0), slope, normed, transposed)
    )
    other = swap(leaving, "c")
    slope, normed, transposed = bring(slope, normed, transposed)

    low, keep, send = backward(
        core, own, other, slope, normed, weight, transposed
    )
    chip_weight, chip_vector = chip_total(keep, swap(send, "c"))

    scale = 1.0 / math.sqrt(DP * SLOTS * BLOCK)
    group_vector = pick(chip_vector, link, 0) + swap(pick(chip_vector, 1 - link, 0), "l")
    terms = lax.all_to_all(
        chip_weight.reshape(2 * DP, 16, LANES), ("dp", "l"), split_axis=0, concat_axis=0, tiled=True
    )
    total = (jnp.sum(terms.astype(jnp.float32), axis=0) * scale).astype(jnp.bfloat16)
    high = lax.reduce_precision(group_vector[:3], 8, 7)
    rest = group_vector[:3] - high
    pair = jnp.concatenate([high, rest]).astype(jnp.bfloat16)
    announce = jnp.concatenate([total, pair, jnp.zeros((2, LANES), jnp.bfloat16)], axis=0)
    heard = lax.all_to_all(
        jnp.broadcast_to(announce, (DP, PAD, LANES)), "dp", split_axis=0, concat_axis=0, tiled=True
    )
    weight_out = heard[:, :16].reshape(2 * channels, LANES).astype(jnp.float32)
    sums = jnp.sum(heard[:, 16:22].astype(jnp.float32), axis=0)
    vector_out = (sums[:3] + sums[3:]) * scale

    own_rows, leaving_rows = input_gradient(core, low, weight)
    chip_rows = jnp.stack([own_rows, swap(leaving_rows, "c")])
    here = pick(chip_rows, link, 1)
    there = swap(pick(chip_rows, 1 - link, 1), "l")
    groups = []
    for part in (0, 1):
        rows = jnp.where(link == part, here, there)
        groups.extend(ordered(core, rows[0], rows[1]))
    grad_feats = (
        jnp.stack(groups)
        .reshape(4, 2, FRAMES, PAD, LANES)[:, :, :, :SLOTS]
        .transpose(3, 0, 2, 1, 4)
        .reshape(feats.shape)
    )
    return (grad_feats, weight_out, vector_out[0], vector_out[1], vector_out[2])


def solution(mesh):
    grid = Mesh(mesh.devices.reshape(DP, 2, 2), ("dp", "l", "c"))
    mp = ("l", "c")
    placed = (
        P("dp", mp),
        P(None, mp),
        P(mp),
        P(mp),
        P(mp),
        P("dp"),
        P("dp", mp),
        P("dp"),
        P("dp"),
    )
    return jax.shard_map(
        on_device,
        mesh=grid,
        in_specs=placed,
        out_specs=(P("dp", mp), P(None, mp), P(mp), P(mp), P(mp)),
        check_vma=False,
    )
```

```python
import math

import jax
import jax.numpy as jnp
import numpy as np
from jax import lax
from jax.experimental import pallas as pl
from jax.experimental.pallas import tpu as pltpu
from jax.sharding import Mesh, PartitionSpec as P

BLOCK = 128
BPU = 7
SLOTS = 21
PAD = 24
DP = 64
LANES = 128
STEPS = 4
FRAMES = 32

MIB = 1024 * 1024
VMEM = 28 * MIB
BRING = 52 * MIB
ALL_VMEM = 60 * MIB

EPSILON = 1e-05
INV_ROOT_TWO = 0.7071067811865476
INV_ROOT_TAU = 0.3989422804014327


def gelu_slope(value):
    return (
        0.5 * (1.0 + lax.erf(value * INV_ROOT_TWO))
        + value * jnp.exp(-0.5 * value * value) * INV_ROOT_TAU
    )


def swap(value, axis):
    return lax.ppermute(value, axis, [(0, 1), (1, 0)])


def pick(array, index, axis):
    return lax.dynamic_index_in_dim(array, index, axis, keepdims=False)


def ordered(flag, mine, other):
    return jnp.where(flag == 0, mine, other), jnp.where(flag == 0, other, mine)


def lay_out_kernel(
    rows_ref, owner_ref, slot_ref, out_ref, held_ref, owners_ref, slots_ref, wide_ref, sems
):
    copies = [
        pltpu.make_async_copy(rows_ref, held_ref, sems.at[0]),
        pltpu.make_async_copy(owner_ref, owners_ref, sems.at[1]),
        pltpu.make_async_copy(slot_ref, slots_ref, sems.at[2]),
    ]
    for copy in copies:
        copy.start()
    wide_ref[(SLOTS + 2) * BLOCK :] = jnp.zeros((BLOCK, LANES), jnp.float32)
    lane = lax.broadcasted_iota(jnp.int32, (1, LANES), 1)
    for place, label_ref in enumerate((owners_ref, slots_ref)):
        copies[1 + place].wait()
        label = jnp.zeros((1, LANES), jnp.int32)
        for block in range(SLOTS):
            label = jnp.where(lane == block, label_ref[block], label)
        start = (SLOTS + place) * BLOCK
        wide_ref[start : start + BLOCK] = jnp.broadcast_to(
            label.astype(jnp.float32), (BLOCK, LANES)
        )
    copies[0].wait()
    wide_ref[: SLOTS * BLOCK] = held_ref[...].astype(jnp.float32)
    for half in range(2):
        for frame in range(DP):
            column = wide_ref[pl.ds(half * DP + frame, PAD, stride=BLOCK), :]
            out_ref[frame, half] = column.astype(jnp.bfloat16)


def lay_out(grad_rows, seg_owner, seg_slot):
    return pl.pallas_call(
        lay_out_kernel,
        out_shape=jax.ShapeDtypeStruct((DP, 2, PAD, LANES), jnp.bfloat16),
        in_specs=[pl.BlockSpec(memory_space=pl.ANY)] * 3,
        scratch_shapes=[
            pltpu.VMEM((SLOTS * BLOCK, LANES), jnp.bfloat16),
            pltpu.SMEM((SLOTS,), jnp.int32),
            pltpu.SMEM((SLOTS,), jnp.int32),
            pltpu.VMEM((PAD * BLOCK, LANES), jnp.float32),
            pltpu.SemaphoreType.DMA((3,)),
        ],
        compiler_params=pltpu.CompilerParams(vmem_limit_bytes=ALL_VMEM),
        cost_estimate=pl.CostEstimate(flops=0, bytes_accessed=1500000, transcendentals=0),
    )(grad_rows, seg_owner, seg_slot)


def permute_kernel(lane_ref, spread_ref, out_ref, rows_ref, labels_ref, target_ref):
    step = pl.program_id(0)
    owners = out_ref.shape[0]
    tile = owners * PAD
    width = DP * PAD

    @pl.when(step == 0)
    def _():
        for half in range(2):
            values = spread_ref[:, half].astype(jnp.float32).reshape(width, LANES)
            rows_ref[:, half * LANES : (half + 1) * LANES] = values.astype(jnp.bfloat16)
        labels_ref[...] = spread_ref[:, 0, PAD - 8 :].astype(jnp.float32).reshape(DP * 8, LANES)
        block = lane_ref[0:1, :]
        source = lane_ref[1:2, :]
        repeat = jnp.where(
            lax.broadcasted_iota(jnp.int32, (LANES, width), 0) == block, 1.0, 0.0
        ).astype(jnp.bfloat16)
        own_row = lax.broadcasted_iota(jnp.int32, (DP, width), 0) == source
        found = []
        for row in (SLOTS, SLOTS + 1):
            label = labels_ref[pl.ds(row - (PAD - 8), DP, stride=8), :].astype(jnp.bfloat16)
            spun = jnp.dot(label, repeat, preferred_element_type=jnp.float32)
            found.append(jnp.sum(jnp.where(own_row, spun, 0.0), axis=0, keepdims=True))
        target = (found[0] * PAD + found[1]).astype(jnp.int32)
        target_ref[...] = jnp.where(block < SLOTS, target, -1)

    wanted = step * tile + lax.broadcasted_iota(jnp.int32, (tile, DP * PAD), 0)
    choose = jnp.where(target_ref[...] == wanted, 1.0, 0.0).astype(jnp.bfloat16)
    moved = jnp.dot(choose, rows_ref[...], preferred_element_type=jnp.float32)
    for half in range(2):
        values = moved[:, half * LANES : (half + 1) * LANES].reshape(owners, PAD, LANES)
        out_ref[:, half] = values.astype(jnp.bfloat16)


def permute_pieces(spread):
    steps = 2
    width = DP * PAD
    lanes = np.arange(width, dtype=np.int32)
    places = np.concatenate([np.stack([lanes % PAD, lanes // PAD]), np.zeros((6, width), np.int32)])
    return pl.pallas_call(
        permute_kernel,
        grid=(steps,),
        out_shape=jax.ShapeDtypeStruct(spread.shape, jnp.bfloat16),
        in_specs=[
            pl.BlockSpec((8, width), lambda i: (0, 0)),
            pl.BlockSpec(spread.shape, lambda i: (0, 0, 0, 0)),
        ],
        out_specs=pl.BlockSpec((DP // steps, 2, PAD, LANES), lambda i: (i, 0, 0, 0)),
        scratch_shapes=[
            pltpu.VMEM((width, 2 * LANES), jnp.bfloat16),
            pltpu.VMEM((DP * 8, LANES), jnp.float32),
            pltpu.VMEM((1, width), jnp.int32),
        ],
        compiler_params=pltpu.CompilerParams(vmem_limit_bytes=VMEM),
        cost_estimate=pl.CostEstimate(
            flops=4 * 2 * width * width * 2 * LANES, bytes_accessed=1600000, transcendentals=0
        ),
    )(places, spread)


def parameter(terms, which):
    terms = terms.astype(jnp.float32)
    return sum(terms[3 * part + which : 3 * part + which + 1] for part in range(3))


def forward_kernel(
    place_ref, lengths_ref, feats_ref, packed_ref, link_ref, beside_ref,
    transposed_ref, slope_ref, normed_ref, weight_ref, rows_ref, wide_ref,
):
    step = pl.program_id(0)
    link, core = place_ref[0], place_ref[1]
    blocks = SLOTS * 2 * FRAMES
    rows, channels = normed_ref.shape
    frames = rows // PAD

    @pl.when(step == 0)
    def _():
        sources = (
            (link * 2 + core, feats_ref[:, 0].astype(jnp.float32).reshape(blocks, LANES), packed_ref[...]),
            (
                (1 - link) * 2 + core,
                link_ref[pl.ds(pl.multiple_of(core * blocks, 16), blocks), :].astype(jnp.float32),
                link_ref[2 * blocks :],
            ),
            (link * 2 + 1 - core, beside_ref[0, :blocks].astype(jnp.float32), beside_ref[0, blocks:]),
            (
                (1 - link) * 2 + 1 - core,
                beside_ref[1, :blocks].astype(jnp.float32),
                beside_ref[1, blocks:],
            ),
        )
        for place, value, weight in sources:
            rows_ref[place, :blocks] = value
            weight_ref[:, pl.ds(pl.multiple_of(place * LANES, LANES), LANES)] = weight
        rows_ref[:, blocks:] = jnp.zeros((4, (PAD - SLOTS) * 2 * FRAMES, LANES), jnp.float32)

    for frame in range(frames):
        for tap in range(2):
            for piece in range(4):
                start = 2 * (step * frames + frame) + tap
                column = tap * channels + piece * LANES
                wide_ref[frame * PAD : (frame + 1) * PAD, column : column + LANES] = rows_ref[
                    piece, pl.ds(start, PAD, stride=2 * FRAMES), :
                ]
    paired = wide_ref[...].astype(jnp.bfloat16)
    transposed_ref[...] = paired.T
    terms = weight_ref[2 * channels :]
    preact = jnp.dot(paired, weight_ref[: 2 * channels], preferred_element_type=jnp.float32)
    preact = preact + parameter(terms, 0)
    centred = preact - jnp.sum(preact, axis=1, keepdims=True) * (1.0 / channels)
    spread = jnp.sum(centred * centred, axis=1, keepdims=True) * (1.0 / channels)
    inv_spread = lax.rsqrt(spread + EPSILON)
    normed = centred * inv_spread
    slope = gelu_slope(normed * parameter(terms, 1) + parameter(terms, 2))
    slot = lax.broadcasted_iota(jnp.int32, (PAD, 1), 0)
    limit = jnp.zeros((PAD, 1), jnp.int32)
    for index in range(SLOTS):
        valid = lax.div(lengths_ref[index // BPU] - 400, 320) + 1
        here = valid - (index % BPU) * BLOCK - (link * 2 + core) * FRAMES
        limit = jnp.where(slot == index, here, limit)
    limits = jnp.concatenate([limit - frame for frame in range(frames)], axis=0)
    slope_ref[:, :channels] = jnp.where(limits > step * frames, slope, 0.0).astype(jnp.bfloat16)
    inv_high = inv_spread.astype(jnp.bfloat16).astype(jnp.float32)
    lower_half = lax.broadcasted_iota(jnp.int32, (rows, LANES), 1) < LANES // 2
    inv_terms = jnp.where(lower_half, inv_high, inv_spread - inv_high)
    slope_ref[:, channels:] = inv_terms.astype(jnp.bfloat16)
    normed_ref[...] = normed.astype(jnp.bfloat16)


def forward(link, core, lengths, feats, packed, from_link, from_core):
    steps = 2
    rows = FRAMES * PAD
    channels = 4 * LANES
    tile = rows // steps
    return pl.pallas_call(
        forward_kernel,
        grid_spec=pltpu.PrefetchScalarGridSpec(
            num_scalar_prefetch=2,
            grid=(steps,),
            in_specs=[
                pl.BlockSpec(
                    (SLOTS, 1, 2 * FRAMES, LANES),
                    lambda i, place, _: (0, 2 * place[0] + place[1], 0, 0),
                ),
                pl.BlockSpec(packed.shape, lambda i, place, _: (0, 0)),
                pl.BlockSpec(from_link.shape, lambda i, place, _: (0, 0)),
                pl.BlockSpec(from_core.shape, lambda i, place, _: (0, 0, 0)),
            ],
            out_specs=(
                pl.BlockSpec((2 * channels, tile), lambda i, place, _: (0, i)),
                pl.BlockSpec((tile, channels + LANES), lambda i, place, _: (i, 0)),
                pl.BlockSpec((tile, channels), lambda i, place, _: (i, 0)),
                pl.BlockSpec((packed.shape[0], channels), lambda i, place, _: (0, 0)),
            ),
            scratch_shapes=[
                pltpu.VMEM((4, PAD * 2 * FRAMES, LANES), jnp.float32),
                pltpu.VMEM((tile, 2 * channels), jnp.float32),
            ],
        ),
        out_shape=(
            pltpu.HBM((2 * channels, rows), jnp.bfloat16),
            pltpu.HBM((rows, channels + LANES), jnp.bfloat16),
            pltpu.HBM((rows, channels), jnp.bfloat16),
            jax.ShapeDtypeStruct((packed.shape[0], channels), jnp.bfloat16),
        ),
        compiler_params=pltpu.CompilerParams(vmem_limit_bytes=VMEM),
        cost_estimate=pl.CostEstimate(
            flops=3 * 4 * rows * channels * channels,
            bytes_accessed=8000000,
            transcendentals=2 * rows * channels,
        ),
    )(jnp.stack([link, core]), lengths, feats, packed, from_link, from_core)


def bring_kernel(slope_hbm, normed_hbm, transposed_hbm, slope_ref, normed_ref, transposed_ref, sems):
    copies = []
    for source, target in (
        (slope_hbm, slope_ref), (normed_hbm, normed_ref), (transposed_hbm, transposed_ref)
    ):
        share = source.shape[0] // 4
        for part in range(4):
            place = pl.ds(part * share, share)
            copies.append(
                pltpu.make_async_copy(source.at[place, :], target.at[place, :], sems.at[len(copies)])
            )
    for copy in copies:
        copy.start()
    for copy in copies:
        copy.wait()


def bring(slope, normed, transposed):
    arrays = (slope, normed, transposed)
    return pl.pallas_call(
        bring_kernel,
        out_shape=tuple(pltpu.VMEM(array.shape, array.dtype) for array in arrays),
        in_specs=[pl.BlockSpec(memory_space=pl.ANY)] * 3,
        out_specs=(pl.BlockSpec(memory_space=pltpu.VMEM),) * 3,
        scratch_shapes=[pltpu.SemaphoreType.DMA((12,))],
        compiler_params=pltpu.CompilerParams(vmem_limit_bytes=BRING),
        cost_estimate=pl.CostEstimate(flops=0, bytes_accessed=10000000, transcendentals=0),
    )(*arrays)


def backward_kernel(
    core_ref, own_ref, other_ref, slope_ref, normed_ref, gain_ref, transposed_ref,
    low_ref, keep_ref, send_ref, sums_ref,
):
    step = pl.program_id(0)
    rows = normed_ref.shape[0]
    here = pl.ds(pl.multiple_of(step * rows, 16), rows)
    first = core_ref[0] == 0
    columns = []
    for link in range(2):
        own = own_ref[0, :, link].astype(jnp.float32).reshape(rows, LANES)
        other = other_ref[:, link].astype(jnp.float32).reshape(rows, LANES)
        columns.append(jnp.where(first, own, other))
        columns.append(jnp.where(first, other, own))
    upstream = jnp.concatenate(columns, axis=1)
    normed = normed_ref[...].astype(jnp.float32)
    channels = normed.shape[1]
    grad_act = upstream * slope_ref[:, :channels].astype(jnp.float32)
    inv_terms = slope_ref[:, channels:].astype(jnp.float32)
    inv_spread = inv_terms[:, :1] + inv_terms[:, LANES // 2 : LANES // 2 + 1]
    weighted = grad_act * normed
    gain = parameter(gain_ref[...], 1)
    grad_normed = grad_act * gain
    grad_mean = jnp.sum(grad_normed, axis=1, keepdims=True) * (1.0 / channels)
    cross_mean = jnp.sum(weighted * gain, axis=1, keepdims=True) * (1.0 / channels)
    grad_pre = inv_spread * (grad_normed - grad_mean - normed * cross_mean)
    low_ref[here, :] = grad_pre.astype(jnp.bfloat16)
    sums = jnp.concatenate(
        [
            jnp.sum(grad_pre, axis=0, keepdims=True),
            jnp.sum(weighted, axis=0, keepdims=True),
            jnp.sum(grad_act, axis=0, keepdims=True),
            jnp.zeros((5, channels), jnp.float32),
        ],
        axis=0,
    )

    @pl.when(step == 0)
    def _():
        sums_ref[...] = sums

    @pl.when(step > 0)
    def _():
        sums_ref[...] += sums

    @pl.when(step == pl.num_programs(0) - 1)
    def _():
        depth = transposed_ref.shape[0]
        for target_ref, which in ((send_ref, 1 - core_ref[0]), (keep_ref, core_ref[0])):
            places = [pl.ds(pl.multiple_of((2 * link + which) * LANES, LANES), LANES) for link in range(2)]
            columns = jnp.concatenate([low_ref[:, place] for place in places], axis=1)
            product = jnp.dot(transposed_ref[...], columns, preferred_element_type=jnp.float32)
            for link in range(2):
                part = product[:, link * LANES : (link + 1) * LANES]
                target_ref[link, :depth] = part.astype(target_ref.dtype)
        for link in range(2):
            kept = pl.ds(pl.multiple_of((2 * link + core_ref[0]) * LANES, LANES), LANES)
            keep_ref[link, depth:] = sums_ref[:, kept]
            sent = pl.ds(pl.multiple_of((2 * link + 1 - core_ref[0]) * LANES, LANES), LANES)
            value = sums_ref[:, sent]
            high = value.astype(jnp.bfloat16).astype(jnp.float32)
            send_ref[link, depth:] = jnp.concatenate([high, value - high], axis=0).astype(
                jnp.bfloat16
            )


def backward(core, own, other, slope, normed, gain, transposed):
    rows, channels = normed.shape
    depth = transposed.shape[0]
    frames = FRAMES // STEPS
    half = jax.ShapeDtypeStruct((2, depth + 8, LANES), jnp.float32)
    leaving = jax.ShapeDtypeStruct((2, depth + 16, LANES), jnp.bfloat16)
    return pl.pallas_call(
        backward_kernel,
        grid_spec=pltpu.PrefetchScalarGridSpec(
            num_scalar_prefetch=1,
            grid=(STEPS,),
            in_specs=[
                pl.BlockSpec((1, frames, 2, PAD, LANES), lambda i, core: (core[0], i, 0, 0, 0)),
                pl.BlockSpec((frames, 2, PAD, LANES), lambda i, core: (i, 0, 0, 0)),
                pl.BlockSpec((rows // STEPS, channels + LANES), lambda i, core: (i, 0)),
                pl.BlockSpec((rows // STEPS, channels), lambda i, core: (i, 0)),
                pl.BlockSpec((16, channels), lambda i, core: (depth // 16, 0)),
                pl.BlockSpec((depth, rows), lambda i, core: (0, 0)),
            ],
            out_specs=(
                pl.BlockSpec((rows, channels), lambda i, core: (0, 0)),
                pl.BlockSpec(half.shape, lambda i, core: (0, 0, 0)),
                pl.BlockSpec(leaving.shape, lambda i, core: (0, 0, 0)),
            ),
            scratch_shapes=[pltpu.VMEM((8, channels), jnp.float32)],
        ),
        out_shape=(jax.ShapeDtypeStruct((rows, channels), jnp.bfloat16), half, leaving),
        compiler_params=pltpu.CompilerParams(vmem_limit_bytes=28 * MIB),
        cost_estimate=pl.CostEstimate(
            flops=2 * rows * depth * channels, bytes_accessed=9000000, transcendentals=0
        ),
    )(core.reshape(1), own, other, slope, normed, gain, transposed)


def input_kernel(core_ref, low_ref, weight_ref, keep_ref, send_ref):
    low = low_ref[...]
    for target_ref, which in ((send_ref, 1 - core_ref[0]), (keep_ref, core_ref[0])):
        for tap in range(2):
            rows = [
                weight_ref[pl.ds(pl.multiple_of((4 * tap + 2 * link + which) * LANES, LANES), LANES), :]
                for link in range(2)
            ]
            product = lax.dot_general(
                low, jnp.concatenate(rows, axis=0), (((1,), (1,)), ((), ())),
                preferred_element_type=jnp.float32,
            ).astype(jnp.bfloat16)
            for link in range(2):
                target_ref[link, tap] = product[:, link * LANES : (link + 1) * LANES]


def input_gradient(core, low, weight):
    rows = low.shape[0]
    half = jax.ShapeDtypeStruct((2, 2, rows, LANES), jnp.bfloat16)
    return pl.pallas_call(
        input_kernel,
        out_shape=(half, half),
        in_specs=[
            pl.BlockSpec(memory_space=pltpu.SMEM),
            pl.BlockSpec(memory_space=pltpu.VMEM),
            pl.BlockSpec(memory_space=pltpu.VMEM),
        ],
        out_specs=(pl.BlockSpec(memory_space=pltpu.VMEM),) * 2,
        compiler_params=pltpu.CompilerParams(vmem_limit_bytes=VMEM),
        cost_estimate=pl.CostEstimate(
            flops=4 * rows * weight.shape[1] * weight.shape[1],
            bytes_accessed=3500000,
            transcendentals=0,
        ),
    )(core.reshape(1), low, weight)


def chip_kernel(keep_ref, other_ref, weight_ref, vector_ref):
    depth = keep_ref.shape[1] - 8
    total = keep_ref[0, :depth] + other_ref[0, :depth].astype(jnp.float32)
    weight_ref[:, 0] = total.reshape(DP, depth // DP, LANES).astype(jnp.bfloat16)
    terms = other_ref[0, depth:].astype(jnp.float32)
    vector_ref[0] = keep_ref[0, depth:] + (terms[:8] + terms[8:])


def chip_total(keep, other):
    depth = keep.shape[1] - 8
    return pl.pallas_call(
        chip_kernel,
        grid=(2,),
        out_shape=(
            jax.ShapeDtypeStruct((DP, 2, depth // DP, LANES), jnp.bfloat16),
            jax.ShapeDtypeStruct((2, 8, LANES), jnp.float32),
        ),
        in_specs=[
            pl.BlockSpec((1, depth + 8, LANES), lambda i: (i, 0, 0)),
            pl.BlockSpec((1, depth + 16, LANES), lambda i: (i, 0, 0)),
        ],
        out_specs=(
            pl.BlockSpec((DP, 1, depth // DP, LANES), lambda i: (0, i, 0, 0)),
            pl.BlockSpec((1, 8, LANES), lambda i: (i, 0, 0)),
        ),
        compiler_params=pltpu.CompilerParams(vmem_limit_bytes=VMEM),
        cost_estimate=pl.CostEstimate(
            flops=2 * depth * LANES, bytes_accessed=2700000, transcendentals=0
        ),
    )(keep, other)


def route(grad_rows, seg_owner, seg_slot):
    outgoing = lay_out(grad_rows, seg_owner, seg_slot)
    spread = lax.all_to_all(outgoing, "dp", split_axis=0, concat_axis=0, tiled=True)
    sorted_pieces = permute_pieces(spread).reshape(2 * DP, PAD, LANES)
    arrived = lax.all_to_all(
        sorted_pieces, ("dp", "l"), split_axis=0, concat_axis=0, tiled=True
    ).reshape(2, FRAMES, 2, PAD, LANES)
    return arrived, sorted_pieces


def pack_parameters(conv_weight, vectors):
    high = lax.reduce_precision(vectors, 8, 7)
    middle = lax.reduce_precision(vectors - high, 8, 7)
    terms = jnp.concatenate([high, middle, vectors - high - middle]).astype(jnp.bfloat16)
    return jnp.concatenate([conv_weight, jnp.pad(terms, ((0, 7), (0, 0)))], axis=0)


def on_device(
    feats, conv_weight, conv_bias, norm_gain, norm_shift, lengths, grad_rows, seg_owner, seg_slot
):
    link, core = lax.axis_index("l"), lax.axis_index("c")
    channels = 4 * LANES

    own, sorted_pieces = route(grad_rows, seg_owner, seg_slot)

    packed = pack_parameters(conv_weight, jnp.stack([conv_bias, norm_gain, norm_shift]))
    by_group = feats.reshape(SLOTS, 2, 2, 2 * FRAMES, LANES).transpose(1, 2, 0, 3, 4)
    by_group = by_group.reshape(2, 2, SLOTS * 2 * FRAMES, LANES)
    away = pick(by_group, 1 - link, 0)
    from_link = swap(jnp.concatenate([away.reshape(-1, LANES), packed]), "l")
    from_link, _ = lax.optimization_barrier((from_link, sorted_pieces))
    rows = SLOTS * 2 * FRAMES
    beside = jnp.stack(
        [
            jnp.concatenate([pick(pick(by_group, link, 0), 1 - core, 0), packed]),
            jnp.concatenate(
                [
                    lax.dynamic_slice_in_dim(from_link, (1 - core) * rows, rows),
                    from_link[2 * rows :],
                ]
            ),
        ]
    )
    from_core = swap(beside, "c")
    transposed, slope, normed, weight = forward(
        link, core, lengths, feats.reshape(SLOTS, 4, 2 * FRAMES, LANES), packed, from_link, from_core
    )

    leaving, slope, normed, transposed = lax.optimization_barrier(
        (pick(own, 1 - core, 0), slope, normed, transposed)
    )
    other = swap(leaving, "c")
    slope, normed, transposed = bring(slope, normed, transposed)

    low, keep, send = backward(
        core, own, other, slope, normed, weight, transposed
    )
    chip_weight, chip_vector = chip_total(keep, swap(send, "c"))

    scale = 1.0 / math.sqrt(DP * SLOTS * BLOCK)
    group_vector = pick(chip_vector, link, 0) + swap(pick(chip_vector, 1 - link, 0), "l")
    terms = lax.all_to_all(
        chip_weight.reshape(2 * DP, 16, LANES), ("dp", "l"), split_axis=0, concat_axis=0, tiled=True
    )
    total = (jnp.sum(terms.astype(jnp.float32), axis=0) * scale).astype(jnp.bfloat16)
    high = lax.reduce_precision(group_vector[:3], 8, 7)
    rest = group_vector[:3] - high
    pair = jnp.concatenate([high, rest]).astype(jnp.bfloat16)
    announce = jnp.concatenate([total, pair, jnp.zeros((2, LANES), jnp.bfloat16)], axis=0)
    heard = lax.all_to_all(
        jnp.broadcast_to(announce, (DP, PAD, LANES)), "dp", split_axis=0, concat_axis=0, tiled=True
    )
    weight_out = heard[:, :16].reshape(2 * channels, LANES).astype(jnp.float32)
    sums = jnp.sum(heard[:, 16:22].astype(jnp.float32), axis=0)
    vector_out = (sums[:3] + sums[3:]) * scale

    own_rows, leaving_rows = input_gradient(core, low, weight)
    chip_rows = jnp.stack([own_rows, swap(leaving_rows, "c")])
    here = pick(chip_rows, link, 1)
    there = swap(pick(chip_rows, 1 - link, 1), "l")
    groups = []
    for part in (0, 1):
        rows = jnp.where(link == part, here, there)
        groups.extend(ordered(core, rows[0], rows[1]))
    grad_feats = (
        jnp.stack(groups)
        .reshape(4, 2, FRAMES, PAD, LANES)[:, :, :, :SLOTS]
        .transpose(3, 0, 2, 1, 4)
        .reshape(feats.shape)
    )
    return (grad_feats, weight_out, vector_out[0], vector_out[1], vector_out[2])


def solution(mesh):
    grid = Mesh(mesh.devices.reshape(DP, 2, 2), ("dp", "l", "c"))
    mp = ("l", "c")
    placed = (
        P("dp", mp),
        P(None, mp),
        P(mp),
        P(mp),
        P(mp),
        P("dp"),
        P("dp", mp),
        P("dp"),
        P("dp"),
    )
    return jax.shard_map(
        on_device,
        mesh=grid,
        in_specs=placed,
        out_specs=(P("dp", mp), P(None, mp), P(mp), P(mp), P(mp)),
        check_vma=False,
    )
```
